32 devices in a mesh: dp: 8 (over z, x), tensor: 4 (over y, core).
Axes of the slice: x: 2, y: 2, z: 4, core: 2. Of those that a mesh axis runs over, the one named last changes fastest.
Arguments:
- tokens_in: bfloat16 [16384, 1024], P(('dp', 'tensor')), may hold values from -6 to 6
- doc_ids: int32 [16384], P('dp'), may hold values from 0 to 15, as said below
- gain_mixer: bfloat16 [1024], replicated, may hold values from 0.25 to 1.75
- in_weight: bfloat16 [1024, 3, 1024], P('dp', None, 'tensor'), may hold values from -0.1875 to 0.1875
- conv_weight: bfloat16 [3, 1024], P(None, 'tensor'), may hold values from -3.5 to 3.5
- out_weight: bfloat16 [1024, 1024], P('tensor', 'dp'), may hold values from -0.1875 to 0.1875
- gain_ffn: bfloat16 [1024], replicated, may hold values from 0.25 to 1.75
- gate_up_weight: bfloat16 [1024, 2, 4608], P('dp', None, 'tensor'), may hold values from -0.1875 to 0.1875
- down_weight: bfloat16 [4608, 1024], P('tensor', 'dp'), may hold values from -0.09375 to 0.09375
- cotangent: bfloat16 [16384, 1024], P(('dp', 'tensor')), may hold values from -6 to 6
Outputs:
- block_out: bfloat16 [16384, 1024], P(('dp', 'tensor'))
- grad_input: float32 [16384, 1024], P(('dp', 'tensor'))
- grad_gain_mixer: float32 [1024], replicated
- grad_in_weight: float32 [1024, 3, 1024], P('dp', None, 'tensor')
- grad_conv_weight: float32 [3, 1024], P(None, 'tensor')
- grad_out_weight: float32 [1024, 1024], P('tensor', 'dp')
- grad_gain_ffn: float32 [1024], replicated
- grad_gate_up: float32 [1024, 2, 4608], P('dp', None, 'tensor')
- grad_down: float32 [4608, 1024], P('tensor', 'dp')
The draws below stay inside these ranges and needn't reach their ends.
Inputs may be any that keep to these rules, and one draw needn't show every extreme that they name: `doc_ids`: document numbers start at 0 at the first token and never fall; each aligned stretch of 1024 tokens after the first holds exactly one document start, never at its first two tokens, and the first stretch holds none.
All inputs are finite; a program needn't handle non-finite values.
Results may differ from the reference program's by a relative error of at most 0.0099.
Values may be sent and summed in bfloat16 or wider, within the bound.
No kernel may reach another device: no remote copies, remote signals or barrier semaphores. Data moves between devices by JAX's collectives and lax.ppermute only.
A program may use at most 192 MiB of HBM per device.

```python
import jax
import jax.numpy as jnp
from jax import lax

D = 1024
FF = 4608
KW = 3
TOK_DEV = 512
DOC_MEAN = 1024
TOKENS = 16384
N_TENSOR = 4


def draw_doc_ids(key, part):
    key = jax.random.fold_in(key, 7)
    stretch_count = TOKENS // DOC_MEAN
    offsets = jax.random.randint(key, (stretch_count,), 2, DOC_MEAN).astype(jnp.int32)
    positions = jnp.arange(TOKENS, dtype=jnp.int32)
    stretch = positions // DOC_MEAN
    places = positions % DOC_MEAN
    starts = jnp.where((places == offsets[stretch]) & (stretch >= 1), 1, 0).astype(jnp.int32)
    return jnp.cumsum(starts).astype(jnp.int32)


def with_spikes(entries, rng, source, target, parts, factor):
    owner, partner = [(jnp.arange(entries.shape[axis_at]) // (entries.shape[axis_at] // parts)).reshape([-1 if axis == axis_at else 1 for axis in range(entries.ndim)]) for axis_at in (source, target)]
    chosen = jax.random.permutation(rng, parts)[partner]
    strong = (owner == chosen) | (owner == (partner + parts // 2) % parts)
    return jnp.where(strong, factor * entries, entries)


def shard_levels(key, extent, cuts, least, largest):
    def one(position, shards_of):
        steps = jax.random.uniform(jax.random.fold_in(jax.random.fold_in(key, 6), position), (shards_of,), jnp.float32, least / len(cuts), largest / len(cuts))
        return jnp.repeat(jnp.exp(steps), extent[position] // shards_of).reshape((-1,) + (1,) * (len(extent) - position - 1))

    gain = one(*cuts[0])
    for cut in cuts[1:]:
        gain = gain * one(*cut)
    return gain


def scatter_about(stream_key, shape, spread, most, cuts=(), kind=jnp.bfloat16):
    entries = spread * jax.random.normal(stream_key, shape, jnp.float32)
    if cuts:
        entries = entries * shard_levels(stream_key, shape, cuts, -0.22, 0.18)
    return jnp.clip(entries, -most, most).astype(kind)


def noise_with(stream_key, dims, width, most, split, heavy, kind=jnp.bfloat16):
    values = width * jax.random.normal(stream_key, dims, jnp.float32)
    if split:
        values = values * shard_levels(stream_key, dims, split, -0.22, 0.18)
    return jnp.clip(with_spikes(values, jax.random.fold_in(stream_key, 3), *heavy), -most, most).astype(kind)


def setup_inputs(seed: int = 0) -> dict:
    splits = jax.random.split(jax.random.key(seed), 11)
    return {
        "tokens_in": noise_with(splits[0], (TOKENS, D), 1.0, 6.0, ((0, 32),), (0, 1, 32, 2.75)),
        "doc_ids": draw_doc_ids(jax.random.fold_in(splits[10], 71), 0),
        "gain_mixer": jnp.clip(1.0 + 0.15 * jax.random.normal(splits[2], (D,), jnp.float32), 0.25, 1.75).astype(jnp.bfloat16),
        "in_weight": scatter_about(splits[3], (D, 3, D), D ** -0.5, 0.1875, ((0, 8), (2, 4))),
        "conv_weight": scatter_about(splits[4], (KW, D), KW ** -0.5, 3.5, ((1, 4),)),
        "out_weight": scatter_about(splits[5], (D, D), D ** -0.5, 0.1875, ((0, 4), (1, 8))),
        "gain_ffn": jnp.clip(1.0 + 0.15 * jax.random.normal(splits[6], (D,), jnp.float32), 0.25, 1.75).astype(jnp.bfloat16),
        "gate_up_weight": scatter_about(splits[7], (D, 2, FF), D ** -0.5, 0.1875, ((0, 8), (2, 4))),
        "down_weight": scatter_about(splits[8], (FF, D), FF ** -0.5, 0.09375, ((0, 4), (1, 8))),
        "cotangent": noise_with(splits[9], (TOKENS, D), 1.0, 6.0, ((0, 32),), (0, 1, 32, 2.75)),
    }


@jax.custom_vjp
def low(v):
    return lax.optimization_barrier(v.astype(jnp.bfloat16)).astype(jnp.float32)

@jax.custom_vjp
def low_back(v):
    return v

def low_keep(v):
    return (low(v), None)

def low_pass(kept, grad):
    return (grad,)

def back_keep(v):
    return (v, None)

def back_low(kept, grad):
    return (low(grad),)
low.defvjp(low_keep, low_pass)
low_back.defvjp(back_keep, back_low)
epsilon = 1e-05

def matmul(left, right):
    return jnp.dot(left, right, precision=lax.Precision.HIGHEST)

def rms_scale(values, gain_vec):
    normed = values * lax.rsqrt(lax.optimization_barrier(jnp.mean(values * values, axis=-1, keepdims=True)) + epsilon)
    return normed * gain_vec

def forward(tokens_in, gain_mixer, in_weight, conv_weight, out_weight, gain_ffn, gate_up_weight, down_weight, doc_ids):
    group_rows = TOK_DEV * N_TENSOR
    blocks_in = tokens_in.reshape(-1, group_rows, D)
    w_in = in_weight.reshape(D, 3 * D)
    w_gu = gate_up_weight.reshape(D, 2 * FF)

    def project_block(block_x):
        hidden_one = low(rms_scale(block_x, gain_mixer))
        return low_back(matmul(hidden_one, w_in))
    projected = lax.map(jax.checkpoint(project_block), blocks_in).reshape(-1, 3 * D)
    b_part = projected[:, :D]
    c_part = projected[:, D:2 * D]
    v_part = projected[:, 2 * D:]
    gated_bx = b_part * v_part
    zero_rows = jnp.zeros((2, D), jnp.float32)
    no_ids = jnp.full((2,), -1, jnp.int32)
    bx_ext = jnp.concatenate([zero_rows, gated_bx], axis=0)
    ids_ext = jnp.concatenate([no_ids, doc_ids.astype(jnp.int32)], axis=0)
    keep_one = (ids_ext[1:-1] == doc_ids).astype(jnp.float32)[:, None]
    keep_two = (ids_ext[:-2] == doc_ids).astype(jnp.float32)[:, None]
    conv_out = conv_weight[0] * gated_bx + conv_weight[1] * keep_one * bx_ext[1:-1] + conv_weight[2] * keep_two * bx_ext[:-2]
    gated = low(c_part * conv_out)
    blocks_gated = gated.reshape(-1, group_rows, D)

    def finish_block(item):
        block_x, block_gated = item
        mixed = low_back(matmul(block_gated, out_weight))
        resid = block_x + mixed
        hidden_two = low(rms_scale(resid, gain_ffn))
        gate_up = low_back(matmul(hidden_two, w_gu))
        gate_part = gate_up[:, :FF]
        up_part = gate_up[:, FF:]
        activated = low(jax.nn.silu(gate_part) * up_part)
        return resid + matmul(activated, down_weight)
    outputs = lax.map(jax.checkpoint(finish_block), (blocks_in, blocks_gated))
    return outputs.reshape(-1, D)

def reference(tokens_in, doc_ids, gain_mixer, in_weight, conv_weight, out_weight, gain_ffn, gate_up_weight, down_weight, cotangent):
    floats = (tokens_in.astype(jnp.float32), gain_mixer.astype(jnp.float32), in_weight.astype(jnp.float32), conv_weight.astype(jnp.float32), out_weight.astype(jnp.float32), gain_ffn.astype(jnp.float32), gate_up_weight.astype(jnp.float32), down_weight.astype(jnp.float32))

    def closed(*params):
        return forward(*params, doc_ids)
    result, pullback = jax.vjp(closed, *floats)
    gradients = pullback(cotangent.astype(jnp.float32))
    return (result.astype(jnp.bfloat16), gradients[0], gradients[1], gradients[2], gradients[3], gradients[4], gradients[5], gradients[6], gradients[7])
```

```python
import jax
import jax.numpy as jnp
from jax import lax
from jax.experimental import pallas as pl
from jax.experimental.pallas import tpu as pltpu
from jax.sharding import PartitionSpec as P

epsilon = 1e-05
HALO = 16
BF = jnp.bfloat16
F32 = jnp.float32


def swap(value, axis, bit):
    peers = lax.axis_size(axis)
    return lax.ppermute(value, axis, [(i, i ^ bit) for i in range(peers)])


def ring(value, axis, by):
    peers = lax.axis_size(axis)
    return lax.ppermute(value, axis, [(i, (i + by) % peers) for i in range(peers)])


def shift(value, by):
    peers = lax.axis_size("dp") * lax.axis_size("tensor")
    pairs = [(i, i + by) for i in range(peers) if 0 <= i + by < peers]
    return lax.ppermute(value, ("dp", "tensor"), pairs)


def nn(left, right):
    return jnp.dot(left, right, preferred_element_type=F32)


def tn(left, right):
    return lax.dot_general(left, right, (((0,), (0,)), ((), ())), preferred_element_type=F32)


def nt(left, right):
    return lax.dot_general(left, right, (((1,), (1,)), ((), ())), preferred_element_type=F32)


def normalize(values):
    scale_vec = lax.rsqrt(jnp.mean(values * values, axis=-1, keepdims=True) + epsilon)
    return (values * scale_vec, scale_vec)


def norm_back(d_normed, normed, scale_vec):
    return scale_vec * (d_normed - normed * jnp.mean(d_normed * normed, axis=-1, keepdims=True))


def reorder(value, order, width):
    rows, columns = value.shape
    if width % 128:
        return value.reshape(rows, -1, width)[:, order].reshape(rows, columns)

    def copy(order_ref, in_ref, out_ref):
        out_ref[...] = in_ref[...]

    return pl.pallas_call(
        copy,
        out_shape=jax.ShapeDtypeStruct(value.shape, value.dtype),
        grid_spec=pltpu.PrefetchScalarGridSpec(
            num_scalar_prefetch=1,
            grid=(columns // width,),
            in_specs=[pl.BlockSpec((rows, width), lambda i, order_ref: (0, order_ref[i]))],
            out_specs=pl.BlockSpec((rows, width), lambda i, order_ref: (0, i)),
        ),
    )(order, value)


def gather_rows(shard):
    pieces = [shard]
    for _ in range(lax.axis_size("dp") // 2 - 1):
        pieces.append(ring(pieces[-1], "dp", 2))
    half = len(pieces) // 2
    near = jnp.concatenate(pieces[:half], axis=0)
    far = jnp.concatenate(pieces[half:], axis=0)
    return [near, far, swap(near, "dp", 1), swap(far, "dp", 1)]


def scatter_rows(total):
    steps = lax.axis_size("dp") // 2
    rows = total.shape[0] // (2 * steps)
    half = steps * rows
    got = swap(total[half:], "dp", 1)

    def part(k):
        return total[k * rows : (k + 1) * rows].astype(F32) + got[k * rows : (k + 1) * rows].astype(F32)

    run = part(steps - 1)
    for k in range(steps - 2, -1, -1):
        run = ring(run.astype(BF), "dp", -2).astype(F32) + part(k)
    return run


def gather_tokens(own):
    other = swap(own, "tensor", 2)
    return jnp.concatenate([own, swap(own, "tensor", 1), other, swap(other, "tensor", 1)], axis=0)


def scatter_tokens(total, rows):
    low = total.astype(BF)
    got_one = swap(low[rows : 2 * rows], "tensor", 1)
    got_three = swap(low[3 * rows :], "tensor", 1)
    far = total[2 * rows : 3 * rows] + got_three.astype(F32)
    got = swap(far.astype(BF), "tensor", 2)
    return total[:rows] + got_one.astype(F32) + got.astype(F32)


def by_xor(groups, me):
    one = jnp.where((me & 1) == 1, groups[jnp.array([1, 0, 3, 2])], groups)
    return jnp.where((me & 2) == 2, one[jnp.array([2, 3, 0, 1])], one)


def sum_all(value):
    for axis in ("tensor", "dp"):
        bit = 1
        while bit < lax.axis_size(axis):
            value = value + swap(value, axis, bit)
            bit *= 2
    return value


def body(
    tokens_in,
    doc_ids,
    gain_mixer,
    in_weight,
    conv_weight,
    out_weight,
    gain_ffn,
    gate_up_weight,
    down_weight,
    cotangent,
):
    rows, width = tokens_in.shape
    dp_count = lax.axis_size("dp")
    block = width // dp_count
    channels = in_weight.shape[2]
    units = gate_up_weight.shape[2]
    me_dp, me_t = lax.axis_index("dp"), lax.axis_index("tensor")
    deep = dp_count // 2
    my_z, my_x = me_dp // 2, me_dp % 2
    index = jnp.arange(dp_count, dtype=jnp.int32)
    order = ((my_z - index % deep) % deep) * 2 + (my_x ^ (index // deep))
    inverse = (my_x ^ (index % 2)) * deep + (my_z - index // 2) % deep

    packed = jnp.concatenate([in_weight.reshape(block, 3 * channels), out_weight.T], axis=1)
    taps_rows = jnp.zeros((HALO, 4 * channels), BF).at[:3, :channels].set(conv_weight)
    mix_own = jnp.concatenate(gather_rows(packed) + [taps_rows], axis=0)
    mix_y = swap(mix_own, "tensor", 2)
    mix = [mix_own, swap(mix_own, "tensor", 1), mix_y, swap(mix_y, "tensor", 1)]
    cut = units // 2 // 128 * 128
    bounds = [(0, cut), (cut, units)]
    ffn = []
    for lo, hi in bounds:
        shard = jnp.concatenate(
            [gate_up_weight[:, 0, lo:hi], gate_up_weight[:, 1, lo:hi], down_weight[lo:hi].T], axis=1
        )
        ffn.append(jnp.concatenate(gather_rows(shard), axis=0))

    last = doc_ids.shape[0]
    ids = jnp.concatenate([doc_ids[:1], doc_ids[:1], doc_ids, doc_ids[last - 1 :], doc_ids[last - 1 :]])
    ids = lax.dynamic_slice(ids, (me_t * rows,), (rows + 4,))
    one_all = (ids[1:] == ids[:-1]).astype(F32)[:, None]
    two_all = (ids[2:] == ids[:-2]).astype(F32)[:, None]
    keep_one, keep_two = one_all[1 : rows + 1], two_all[:rows]
    next_one, next_two = one_all[2 : rows + 2], two_all[2 : rows + 2]
    tail = tokens_in[rows - HALO :]
    linked = (ids[rows] == ids[rows + 1]).astype(BF)
    tail = tail * jnp.ones((HALO, 1), BF).at[HALO - 2, 0].set(linked)
    extended = jnp.concatenate([shift(tail, 1), tokens_in], axis=0)
    extended = reorder(extended, order, block)
    cot = reorder(cotangent, order, block)
    gains = reorder(jnp.stack([gain_mixer, gain_ffn]), order, block).astype(F32)
    gain_one, gain_two = gains[:1], gains[1:]
    cot_full = gather_tokens(cot)

    normed_ext, scale_ext = normalize(extended.astype(F32))
    hidden_ext = (normed_ext * gain_one).astype(BF)
    normed_one, scale_one = normed_ext[HALO:], scale_ext[HALO:]
    hidden_one = hidden_ext[HALO:]
    tokens_f = extended[HALO:].astype(F32)

    saved = []
    mixed = tokens_f
    for group in mix:
        taps = group[width : width + 3, :channels].astype(F32)
        projected = nn(hidden_ext, group[:width, : 3 * channels])
        b_part = projected[:, :channels]
        c_part = projected[HALO:, channels : 2 * channels]
        v_part = projected[:, 2 * channels :]
        bx = b_part * v_part
        bx0, bx1, bx2 = bx[HALO:], keep_one * bx[HALO - 1 : -1], keep_two * bx[HALO - 2 : -2]
        conv_out = taps[0] * bx0 + taps[1] * bx1 + taps[2] * bx2
        gated = (c_part * conv_out).astype(BF)
        mixed = mixed + nt(gated, group[:width, 3 * channels :])
        saved.append((b_part[HALO:], c_part, v_part[HALO:], bx0, bx1, bx2, conv_out, gated, taps))
    resid = mixed
    normed_two, scale_two = normalize(resid)
    hidden_two = (normed_two * gain_two).astype(BF)
    hidden_full = gather_tokens(hidden_two)

    out_sum = d_sum = 0.0
    ffn_grads = []
    for weights, (lo, hi) in zip(ffn, bounds):
        size = hi - lo
        w_gu, w_down = weights[:, : 2 * size], weights[:, 2 * size :]
        gate_up = nn(hidden_full, w_gu)
        d_act = nn(cot_full, w_down)
        gate, up = gate_up[:, :size], gate_up[:, size:]
        sigma = jax.nn.sigmoid(gate)
        silu = gate * sigma
        act = (silu * up).astype(BF)
        d_gate = d_act * up * sigma * (1.0 + gate * (1.0 - sigma))
        d_gu = jnp.concatenate([d_gate, d_act * silu], axis=1).astype(BF)
        d_sum = d_sum + nt(d_gu, w_gu)
        out_sum = out_sum + nt(act, w_down)
        grads = jnp.concatenate(
            [tn(hidden_full, d_gu).astype(BF), tn(cot_full, act).astype(BF)], axis=1
        )
        ffn_grads.append(scatter_rows(grads))
    d_hidden_two = scatter_tokens(d_sum, rows)
    block_out = reorder((resid + scatter_tokens(out_sum, rows)).astype(BF), inverse, block)

    part_gain_two = jnp.sum(d_hidden_two * normed_two, axis=0)
    d_resid = cot.astype(F32) + norm_back(d_hidden_two * gain_two, normed_two, scale_two)
    d_mix = d_resid.astype(BF)

    d_gated = [nn(d_mix, group[:width, 3 * channels :]) for group in mix]
    d_conv = [back * keep[1] for back, keep in zip(d_gated, saved)]
    first = by_xor(jnp.stack([value[:2] for value in d_conv]), me_t)
    following = by_xor(shift(first, -1), me_t)
    d_hidden_one = 0.0
    conv_parts, mix_grads = [], []
    for r, group in enumerate(mix):
        b_part, c_part, v_part, bx0, bx1, bx2, conv_out, gated, taps = saved[r]
        conv_parts.append(jnp.stack([jnp.sum(v * d_conv[r], axis=0) for v in (bx0, bx1, bx2)]))
        ahead = jnp.concatenate([d_conv[r], following[r]], axis=0)
        d_bx = (
            taps[0] * d_conv[r]
            + taps[1] * next_one * ahead[1 : rows + 1]
            + taps[2] * next_two * ahead[2:]
        )
        d_proj = jnp.concatenate(
            [d_bx * v_part, d_gated[r] * conv_out, d_bx * b_part], axis=1
        ).astype(BF)
        d_hidden_one = d_hidden_one + nt(d_proj, group[:width, : 3 * channels])
        mix_grads.append(
            jnp.concatenate([tn(hidden_one, d_proj).astype(BF), tn(d_mix, gated).astype(BF)], axis=1)
        )
    part_gain_one = jnp.sum(d_hidden_one * normed_one, axis=0)
    grad_input = d_resid + norm_back(d_hidden_one * gain_one, normed_one, scale_one)
    grad_input = reorder(grad_input, inverse, block)

    far = mix_grads[2].astype(F32) + swap(mix_grads[3], "tensor", 1).astype(F32)
    near = mix_grads[0].astype(F32) + swap(mix_grads[1], "tensor", 1).astype(F32)
    mix_sum = scatter_rows((near + swap(far.astype(BF), "tensor", 2).astype(F32)).astype(BF))

    conv_all = by_xor(jnp.stack(conv_parts), me_t)
    gain_parts = reorder(jnp.stack([part_gain_one, part_gain_two]), inverse, block)
    small = jnp.concatenate([gain_parts.reshape(2, 4, channels), conv_all.transpose(1, 0, 2)], axis=0)
    small = sum_all(small.reshape(small.shape[0], width))
    grad_conv = lax.dynamic_slice(small, (2, me_t * channels), (small.shape[0] - 2, channels))

    grad_in = mix_sum[:, : 3 * channels].reshape(block, 3, channels)
    grad_out = mix_sum[:, 3 * channels :].T
    grad_gu, grad_down = [], []
    for part, (lo, hi) in zip(ffn_grads, bounds):
        size = hi - lo
        grad_gu.append(part[:, : 2 * size].reshape(block, 2, size))
        grad_down.append(part[:, 2 * size :].T)
    return (
        block_out,
        grad_input,
        small[0],
        grad_in,
        grad_conv,
        grad_out,
        small[1],
        jnp.concatenate(grad_gu, axis=2),
        jnp.concatenate(grad_down, axis=0),
    )


def solution(mesh):
    return jax.shard_map(
        body,
        mesh=mesh,
        in_specs=(
            P(("dp", "tensor"), None),
            P("dp"),
            P(),
            P("dp", None, "tensor"),
            P(None, "tensor"),
            P("tensor", "dp"),
            P(),
            P("dp", None, "tensor"),
            P("tensor", "dp"),
            P(("dp", "tensor"), None),
        ),
        out_specs=(
            P(("dp", "tensor"), None),
            P(("dp", "tensor"), None),
            P(),
            P("dp", None, "tensor"),
            P(None, "tensor"),
            P("tensor", "dp"),
            P(),
            P("dp", None, "tensor"),
            P("tensor", "dp"),
        ),
        check_vma=False,
    )
```

```python
import jax
import jax.numpy as jnp
from jax import lax
from jax.experimental import pallas as pl
from jax.experimental.pallas import tpu as pltpu
from jax.sharding import PartitionSpec as P

epsilon = 1e-05
HALO = 16
LONG = 8
BF = jnp.bfloat16
F32 = jnp.float32


def swap(value, axis, bit):
    peers = lax.axis_size(axis)
    return lax.ppermute(value, axis, [(i, i ^ bit) for i in range(peers)])


def ring(value, axis, by):
    peers = lax.axis_size(axis)
    return lax.ppermute(value, axis, [(i, (i + by) % peers) for i in range(peers)])


def shift(value, by):
    peers = lax.axis_size("dp") * lax.axis_size("tensor")
    pairs = [(i, i + by) for i in range(peers) if 0 <= i + by < peers]
    return lax.ppermute(value, ("dp", "tensor"), pairs)


def nn(left, right):
    return jnp.dot(left, right, preferred_element_type=F32)


def tn(left, right):
    return lax.dot_general(left, right, (((0,), (0,)), ((), ())), preferred_element_type=F32)


def nt(left, right):
    return lax.dot_general(left, right, (((1,), (1,)), ((), ())), preferred_element_type=F32)


def normalize(values):
    scale_vec = lax.rsqrt(jnp.mean(values * values, axis=-1, keepdims=True) + epsilon)
    return (values * scale_vec, scale_vec)


def norm_back(d_normed, normed, scale_vec):
    return scale_vec * (d_normed - normed * jnp.mean(d_normed * normed, axis=-1, keepdims=True))


def after(value, *others):
    return lax.optimization_barrier((value,) + others)[0]


def reorder(values, perm):
    return nn(values, perm).astype(BF)


def reorder_f32(values, perm):
    high = lax.optimization_barrier(values.astype(BF))
    low = (values - high.astype(F32)).astype(BF)
    return nn(high, perm) + nn(low, perm)


def blocks_order():
    steps, me = lax.axis_size("dp") // 2, lax.axis_index("dp")
    index = jnp.arange(2 * steps, dtype=jnp.int32)
    return ((me // 2 - index // 2) % steps) * 2 + ((me % 2) ^ (index % 2))


def ring_gather(shard):
    steps = lax.axis_size("dp") // 2
    if steps > LONG:
        whole = lax.all_gather(shard, "dp", axis=0)[blocks_order()]
        return [[whole.reshape(-1, shard.shape[1])]]
    here = [shard]
    for _ in range(steps - 1):
        here.append(ring(here[-1], "dp", 2))
    return [(piece, swap(piece, "dp", 1)) for piece in here]


def scatter_rows(total):
    steps = lax.axis_size("dp") // 2
    rows = total.shape[0] // (2 * steps)
    if steps > LONG:
        total = total.reshape(2 * steps, rows, -1)[blocks_order()].reshape(total.shape)
        return lax.psum_scatter(total, "dp", scatter_dimension=0, tiled=True).astype(F32)

    def part(k):
        low = 2 * k * rows
        got = swap(total[low + rows : low + 2 * rows], "dp", 1)
        return total[low : low + rows].astype(F32) + got.astype(F32)

    run = part(steps - 1)
    for k in range(steps - 2, -1, -1):
        run = ring(run.astype(BF), "dp", -2).astype(F32) + part(k)
    return run


def ffn(hidden, cot, weights, before, tile):
    rows, width = hidden.shape
    size = weights.shape[1] // 3

    def kernel(*refs):
        h_ref, g_ref, w_ref = refs[:3]
        d_ref, o_ref, d_gu_ref, act_ref = refs[-4:]
        gate_up = nn(h_ref[...], w_ref[:, : 2 * size])
        d_act = nn(g_ref[...], w_ref[:, 2 * size :])
        gate, up = gate_up[:, :size], gate_up[:, size:]
        sigma = 1.0 / (1.0 + jnp.exp(-gate))
        silu = gate * sigma
        act = (silu * up).astype(BF)
        act_ref[...] = act
        d_gu_ref[:, :size] = (d_act * up * (sigma * (1.0 + gate * (1.0 - sigma)))).astype(BF)
        d_gu_ref[:, size:] = (d_act * silu).astype(BF)
        d_sum = nt(d_gu_ref[...], w_ref[:, : 2 * size])
        o_sum = nt(act, w_ref[:, 2 * size :])
        if before:
            d_sum = d_sum + refs[3][...]
            o_sum = o_sum + refs[4][...]
        d_ref[...] = d_sum.astype(d_ref.dtype)
        o_ref[...] = o_sum.astype(o_ref.dtype)

    tokens = pl.BlockSpec((tile, width), lambda i: (i, 0))
    kind = BF if before else F32
    return pl.pallas_call(
        kernel,
        grid=(rows // tile,),
        in_specs=[tokens, tokens, pl.BlockSpec(weights.shape, lambda i: (0, 0))] + [tokens] * len(before),
        out_specs=[
            tokens,
            tokens,
            pl.BlockSpec((tile, 2 * size), lambda i: (i, 0)),
            pl.BlockSpec((tile, size), lambda i: (i, 0)),
        ],
        out_shape=[
            jax.ShapeDtypeStruct((rows, width), kind),
            jax.ShapeDtypeStruct((rows, width), kind),
            jax.ShapeDtypeStruct((rows, 2 * size), BF),
            jax.ShapeDtypeStruct((rows, size), BF),
        ],
        compiler_params=pltpu.CompilerParams(vmem_limit_bytes=48 << 20),
        cost_estimate=pl.CostEstimate(
            flops=12 * rows * width * size,
            bytes_accessed=rows * width * 12 + weights.size * 2,
            transcendentals=rows * size,
        ),
    )(hidden, cot, weights, *before)


def by_xor(groups, me):
    one = [jnp.where((me & 1) == 1, groups[i ^ 1], groups[i]) for i in range(4)]
    return [jnp.where((me & 2) == 2, one[i ^ 2], one[i]) for i in range(4)]


def sum_all(value):
    for axis in ("tensor", "dp"):
        bit = 1
        while bit < lax.axis_size(axis):
            value = value + swap(value, axis, bit)
            bit *= 2
    return value


def body(
    tokens_in,
    doc_ids,
    gain_mixer,
    in_weight,
    conv_weight,
    out_weight,
    gain_ffn,
    gate_up_weight,
    down_weight,
    cotangent,
):
    rows, width = tokens_in.shape
    dp_count = lax.axis_size("dp")
    block = width // dp_count
    channels = in_weight.shape[2]
    units = gate_up_weight.shape[2]
    me_t = lax.axis_index("tensor")
    deep = dp_count // 2

    lane = jnp.arange(width, dtype=jnp.int32)
    source = jnp.repeat(blocks_order(), block) * block + lane % block
    perm = (lane[:, None] == source[None, :]).astype(BF)

    tail = tokens_in[rows - HALO :]
    linked = (doc_ids[(me_t + 1) * rows - 2] == doc_ids[(me_t + 1) * rows - 1]).astype(BF)
    tail = tail * jnp.ones((HALO, 1), BF).at[HALO - 2, 0].set(linked)
    halo = shift(tail, 1)

    packed = jnp.concatenate([in_weight.reshape(block, 3 * channels), out_weight.T], axis=1)
    taps_rows = jnp.zeros((HALO, 4 * channels), BF).at[:3, :channels].set(conv_weight)
    pairs = ring_gather(packed)
    own_pieces, y_pieces = [], []
    for k, pair in enumerate(pairs):
        piece = jnp.concatenate(list(pair) + ([taps_rows] if k == len(pairs) - 1 else []), axis=0)
        own_pieces.append(piece)
        y_pieces.append(swap(piece, "tensor", 2))
    mix_own, mix_y = jnp.concatenate(own_pieces, axis=0), jnp.concatenate(y_pieces, axis=0)
    mix = [mix_own, swap(mix_own, "tensor", 1), mix_y, swap(mix_y, "tensor", 1)]
    cut = units // 2 // 128 * 128
    bounds = [(0, cut), (cut, units)]
    blocks = []
    waits_for = pairs[-1][0]
    for lo, hi in bounds:
        shard = jnp.concatenate(
            [gate_up_weight[:, 0, lo:hi], gate_up_weight[:, 1, lo:hi], down_weight[lo:hi].T], axis=1
        )
        pieces = ring_gather(after(shard, waits_for))
        waits_for = pieces[len(pieces) // 2][0]
        blocks.append(jnp.concatenate([piece for pair in pieces for piece in pair], axis=0))

    last = doc_ids.shape[0]
    ids = jnp.concatenate([doc_ids[:1], doc_ids[:1], doc_ids, doc_ids[last - 1 :], doc_ids[last - 1 :]])
    ids = lax.dynamic_slice(ids, (me_t * rows,), (rows + 4,))
    one_all = (ids[1:] == ids[:-1]).astype(F32)[:, None]
    two_all = (ids[2:] == ids[:-2]).astype(F32)[:, None]
    keep_one, keep_two = one_all[1 : rows + 1], two_all[:rows]
    next_one, next_two = one_all[2 : rows + 2], two_all[2 : rows + 2]
    cot = reorder(cotangent, perm)
    gains = reorder(jnp.stack([gain_mixer, gain_ffn]), perm).astype(F32)
    gain_one, gain_two = gains[:1], gains[1:]
    cot_y = swap(after(cot, y_pieces[-1]), "tensor", 2)
    cot_c, cot_yc = swap(cot, "tensor", 1), swap(cot_y, "tensor", 1)
    extended = reorder(jnp.concatenate([halo, tokens_in], axis=0), perm)

    normed_ext, scale_ext = normalize(extended.astype(F32))
    hidden_ext = (normed_ext * gain_one).astype(BF)
    normed_one, scale_one = normed_ext[HALO:], scale_ext[HALO:]
    hidden_one = hidden_ext[HALO:]
    tokens_f = extended[HALO:].astype(F32)

    saved = []
    mixed = tokens_f
    for group in mix:
        taps = group[width : width + 3, :channels].astype(F32)
        projected = nn(hidden_ext, group[:width, : 3 * channels])
        b_part = projected[:, :channels]
        c_part = projected[HALO:, channels : 2 * channels]
        v_part = projected[:, 2 * channels :]
        bx = b_part * v_part
        bx0, bx1, bx2 = bx[HALO:], keep_one * bx[HALO - 1 : -1], keep_two * bx[HALO - 2 : -2]
        conv_out = taps[0] * bx0 + taps[1] * bx1 + taps[2] * bx2
        gated = (c_part * conv_out).astype(BF)
        mixed = mixed + nt(gated, group[:width, 3 * channels :])
        saved.append((b_part[HALO:], c_part, v_part[HALO:], bx0, bx1, bx2, conv_out, gated, taps))
    resid = mixed
    normed_two, scale_two = normalize(resid)
    hidden_two = (normed_two * gain_two).astype(BF)
    hid_y = swap(hidden_two, "tensor", 2)
    hid_c, hid_yc = swap(hidden_two, "tensor", 1), swap(hid_y, "tensor", 1)
    hid = [jnp.concatenate([hidden_two, hid_c], axis=0), jnp.concatenate([hid_y, hid_yc], axis=0)]
    cots = [jnp.concatenate([cot, cot_c], axis=0), jnp.concatenate([cot_y, cot_yc], axis=0)]
    hid_all, cot_all = jnp.concatenate(hid, axis=0), jnp.concatenate(cots, axis=0)

    tile = min(rows, 256)

    def weight_grads(near, far):
        d_gu, act = (jnp.concatenate([near[i], far[i]], axis=0) for i in (2, 3))
        grads = [tn(hid_all, d_gu).astype(BF), tn(cot_all, act).astype(BF)]
        return scatter_rows(jnp.concatenate(grads, axis=1))

    near = ffn(hid[0], cots[0], blocks[0], (), tile)
    far = ffn(hid[1], cots[1], blocks[0], (), tile)
    ffn_grads = [weight_grads(near, far)]
    far_two = ffn(hid[1], cots[1], blocks[1], tuple(far[:2]), tile)
    near_two = ffn(hid[0], cots[0], blocks[1], tuple(near[:2]), tile)
    ffn_grads.append(weight_grads(near_two, far_two))

    def core_sum(total):
        return total[:rows].astype(F32) + swap(total[rows:], "tensor", 1).astype(F32)

    d_y = swap(core_sum(far_two[0]).astype(BF), "tensor", 2)
    d_hidden_two = core_sum(near_two[0]) + d_y.astype(F32)
    out_far = after(core_sum(far_two[1]).astype(BF), d_y)
    out_own = core_sum(near_two[1]) + swap(out_far, "tensor", 2).astype(F32)
    block_out = reorder((resid + out_own).astype(BF), perm)

    part_gain_two = jnp.sum(d_hidden_two * normed_two, axis=0)
    d_resid = cot.astype(F32) + norm_back(d_hidden_two * gain_two, normed_two, scale_two)
    d_mix = d_resid.astype(BF)

    d_gated = [nn(d_mix, group[:width, 3 * channels :]) for group in mix]
    d_conv = [back * keep[1] for back, keep in zip(d_gated, saved)]
    first = jnp.stack(by_xor([value[:2] for value in d_conv], me_t))
    following = shift(first, -1)
    following = by_xor([following[i] for i in range(4)], me_t)
    conv_parts, mix_grads, d_projs = [], [], []
    for r in range(4):
        b_part, c_part, v_part, bx0, bx1, bx2, conv_out, gated, taps = saved[r]
        conv_parts.append(jnp.stack([jnp.sum(v * d_conv[r], axis=0) for v in (bx0, bx1, bx2)]))
        ahead = jnp.concatenate([d_conv[r], following[r]], axis=0)
        d_bx = (
            taps[0] * d_conv[r]
            + taps[1] * next_one * ahead[1 : rows + 1]
            + taps[2] * next_two * ahead[2:]
        )
        d_proj = jnp.concatenate(
            [d_bx * v_part, d_gated[r] * conv_out, d_bx * b_part], axis=1
        ).astype(BF)
        d_projs.append(d_proj)
        mix_grads.append([tn(hidden_one, d_proj).astype(BF), tn(d_mix, gated).astype(BF)])

    half = 2 * channels

    def columns(grads):
        return [grads[0][:, :half], jnp.concatenate([grads[0][:, half:], grads[1]], axis=1)]

    parts = [columns(grads) for grads in mix_grads]
    near, far = (
        [parts[i][j].astype(F32) + swap(parts[i + 1][j], "tensor", 1).astype(F32) for j in (0, 1)]
        for i in (0, 2)
    )

    def by_x(values):
        return values.reshape(deep, 2, block, half)

    got = by_x(near[0] + swap(far[0].astype(BF), "tensor", 2).astype(F32))
    sum_left = got[:, 0] + swap(got[:, 1].astype(BF), "dp", 1).astype(F32)
    both = jnp.stack([by_x(near[1]), by_x(far[1])])
    both = both[:, :, 0] + swap(both[:, :, 1].astype(BF), "dp", 1).astype(F32)
    sum_right = both[0] + swap(both[1].astype(BF), "tensor", 2).astype(F32)
    total = jnp.concatenate([sum_left, sum_right], axis=2)
    mix_sum = total[0]
    for k in range(1, deep):
        mix_sum = mix_sum + ring(total[k].astype(BF), "dp", -2 * k).astype(F32)

    d_hidden_one = 0.0
    for r, group in enumerate(mix):
        d_hidden_one = d_hidden_one + nt(d_projs[r], group[:width, : 3 * channels])
    part_gain_one = jnp.sum(d_hidden_one * normed_one, axis=0)
    grad_input = d_resid + norm_back(d_hidden_one * gain_one, normed_one, scale_one)
    grad_input = reorder_f32(grad_input, perm)

    conv_all = jnp.stack(by_xor(conv_parts, me_t), axis=1)
    gain_parts = reorder_f32(jnp.stack([part_gain_one, part_gain_two]), perm)
    small = sum_all(jnp.concatenate([gain_parts, conv_all.reshape(-1, width)], axis=0))
    grad_conv = lax.dynamic_slice(small, (2, me_t * channels), (small.shape[0] - 2, channels))

    grad_in = mix_sum[:, : 3 * channels].reshape(block, 3, channels)
    grad_out = mix_sum[:, 3 * channels :].T
    grad_gu, grad_down = [], []
    for part, (lo, hi) in zip(ffn_grads, bounds):
        size = hi - lo
        grad_gu.append(part[:, : 2 * size].reshape(block, 2, size))
        grad_down.append(part[:, 2 * size :].T)
    return (
        block_out,
        grad_input,
        small[0],
        grad_in,
        grad_conv,
        grad_out,
        small[1],
        jnp.concatenate(grad_gu, axis=2),
        jnp.concatenate(grad_down, axis=0),
    )


def solution(mesh):
    return jax.shard_map(
        body,
        mesh=mesh,
        in_specs=(
            P(("dp", "tensor"), None),
            P("dp"),
            P(),
            P("dp", None, "tensor"),
            P(None, "tensor"),
            P("tensor", "dp"),
            P(),
            P("dp", None, "tensor"),
            P("tensor", "dp"),
            P(("dp", "tensor"), None),
        ),
        out_specs=(
            P(("dp", "tensor"), None),
            P(("dp", "tensor"), None),
            P(),
            P("dp", None, "tensor"),
            P(None, "tensor"),
            P("tensor", "dp"),
            P(),
            P("dp", None, "tensor"),
            P("tensor", "dp"),
        ),
        check_vma=False,
    )
```

```python
import jax
import jax.numpy as jnp
from jax import lax
from jax.experimental import pallas as pl
from jax.experimental.pallas import tpu as pltpu
from jax.sharding import PartitionSpec as P

epsilon = 1e-05
HALO = 16
LONG = 8
BF = jnp.bfloat16
F32 = jnp.float32


def swap(value, axis, bit):
    peers = lax.axis_size(axis)
    return lax.ppermute(value, axis, [(i, i ^ bit) for i in range(peers)])


def ring(value, axis, by):
    peers = lax.axis_size(axis)
    return lax.ppermute(value, axis, [(i, (i + by) % peers) for i in range(peers)])


def shift(value, by):
    peers = lax.axis_size("dp") * lax.axis_size("tensor")
    pairs = [(i, i + by) for i in range(peers) if 0 <= i + by < peers]
    return lax.ppermute(value, ("dp", "tensor"), pairs)


def nn(left, right):
    return jnp.dot(left, right, preferred_element_type=F32)


def tn(left, right):
    return lax.dot_general(left, right, (((0,), (0,)), ((), ())), preferred_element_type=F32)


def nt(left, right):
    return lax.dot_general(left, right, (((1,), (1,)), ((), ())), preferred_element_type=F32)


def normalize(values):
    scale_vec = lax.rsqrt(jnp.mean(values * values, axis=-1, keepdims=True) + epsilon)
    return (values * scale_vec, scale_vec)


def norm_back(d_normed, normed, scale_vec):
    return scale_vec * (d_normed - normed * jnp.mean(d_normed * normed, axis=-1, keepdims=True))


def after(value, *others):
    return lax.optimization_barrier((value,) + others)[0]


def reorder(values, perm):
    return nn(values, perm).astype(BF)


def reorder_f32(values, perm):
    high = lax.optimization_barrier(values.astype(BF))
    low = (values - high.astype(F32)).astype(BF)
    return nn(high, perm) + nn(low, perm)


def blocks_order():
    steps, me = lax.axis_size("dp") // 2, lax.axis_index("dp")
    index = jnp.arange(2 * steps, dtype=jnp.int32)
    order = ((me // 2 - index % steps) % steps) * 2 + ((me % 2) ^ (index // steps))
    inverse = ((index % 2) ^ (me % 2)) * steps + (me // 2 - index // 2) % steps
    return order, inverse


def long_gather(shard):
    whole = lax.all_gather(shard, "dp", axis=0)[blocks_order()[0]]
    return whole.reshape(-1, shard.shape[1])


def long_scatter(near, far):
    total = jnp.concatenate([near, far], axis=0)
    peers = lax.axis_size("dp")
    total = total.reshape(peers, total.shape[0] // peers, -1)[blocks_order()[1]].reshape(total.shape)
    return lax.psum_scatter(total, "dp", scatter_dimension=0, tiled=True).astype(F32)


def chain(shard):
    here = [shard]
    for _ in range(lax.axis_size("dp") // 2 - 1):
        here.append(ring(here[-1], "dp", 2))
    return here


def others(here):
    return [swap(piece, "dp", 1) for piece in here]


def ffn(hidden, cot, weights, before, tile):
    rows, width = hidden.shape
    size = weights.shape[1] // 3

    def kernel(*refs):
        h_ref, g_ref, w_ref = refs[:3]
        d_ref, o_ref, d_gu_ref, act_ref = refs[-4:]
        gate_up = nn(h_ref[...], w_ref[:, : 2 * size])
        d_act = nn(g_ref[...], w_ref[:, 2 * size :])
        gate, up = gate_up[:, :size], gate_up[:, size:]
        sigma = 1.0 / (1.0 + jnp.exp(-gate))
        silu = gate * sigma
        act = (silu * up).astype(BF)
        act_ref[...] = act
        d_gu_ref[:, :size] = (d_act * up * (sigma * (1.0 + gate * (1.0 - sigma)))).astype(BF)
        d_gu_ref[:, size:] = (d_act * silu).astype(BF)
        d_sum = nt(d_gu_ref[...], w_ref[:, : 2 * size])
        o_sum = nt(act, w_ref[:, 2 * size :])
        if before:
            d_sum = d_sum + refs[3][...]
            o_sum = o_sum + refs[4][...]
        d_ref[...] = d_sum.astype(d_ref.dtype)
        o_ref[...] = o_sum.astype(o_ref.dtype)

    tokens = pl.BlockSpec((tile, width), lambda i: (i, 0))
    kind = BF if before else F32
    return pl.pallas_call(
        kernel,
        grid=(rows // tile,),
        in_specs=[tokens, tokens, pl.BlockSpec(weights.shape, lambda i: (0, 0))] + [tokens] * len(before),
        out_specs=[
            tokens,
            tokens,
            pl.BlockSpec((tile, 2 * size), lambda i: (i, 0)),
            pl.BlockSpec((tile, size), lambda i: (i, 0)),
        ],
        out_shape=[
            jax.ShapeDtypeStruct((rows, width), kind),
            jax.ShapeDtypeStruct((rows, width), kind),
            jax.ShapeDtypeStruct((rows, 2 * size), BF),
            jax.ShapeDtypeStruct((rows, size), BF),
        ],
        compiler_params=pltpu.CompilerParams(vmem_limit_bytes=48 << 20),
        cost_estimate=pl.CostEstimate(
            flops=12 * rows * width * size,
            bytes_accessed=rows * width * 12 + weights.size * 2,
            transcendentals=rows * size,
        ),
    )(hidden, cot, weights, *before)


def by_xor(groups, me):
    one = [jnp.where((me & 1) == 1, groups[i ^ 1], groups[i]) for i in range(4)]
    return [jnp.where((me & 2) == 2, one[i ^ 2], one[i]) for i in range(4)]


def sum_all(value):
    for axis in ("tensor", "dp"):
        bit = 1
        while bit < lax.axis_size(axis):
            value = value + swap(value, axis, bit)
            bit *= 2
    return value


def body(
    tokens_in,
    doc_ids,
    gain_mixer,
    in_weight,
    conv_weight,
    out_weight,
    gain_ffn,
    gate_up_weight,
    down_weight,
    cotangent,
):
    rows, width = tokens_in.shape
    dp_count = lax.axis_size("dp")
    block = width // dp_count
    channels = in_weight.shape[2]
    units = gate_up_weight.shape[2]
    me_t = lax.axis_index("tensor")
    deep = dp_count // 2
    half = width // 2
    long = deep > LONG

    tail = tokens_in[rows - HALO :]
    linked = (doc_ids[(me_t + 1) * rows - 2] == doc_ids[(me_t + 1) * rows - 1]).astype(BF)
    tail = tail * jnp.ones((HALO, 1), BF).at[HALO - 2, 0].set(linked)
    halo = shift(tail, 1)

    packed = jnp.concatenate(
        [in_weight[:, 0], in_weight[:, 2], in_weight[:, 1], out_weight.T], axis=1
    )
    taps_rows = jnp.zeros((HALO, 4 * channels), BF).at[:3, :channels].set(conv_weight)
    cut = units // 2 // 128 * 128
    bounds = [(0, cut), (cut, units)]

    def pack(lo, hi, *earlier):
        gate_up, down = lax.optimization_barrier((gate_up_weight, down_weight) + earlier)[:2]
        return jnp.concatenate([gate_up[:, 0, lo:hi], gate_up[:, 1, lo:hi], down[lo:hi].T], axis=1)

    if long:
        whole = jnp.concatenate([long_gather(packed), taps_rows], axis=0)
        whole_y = swap(whole, "tensor", 2)
        blocks = [long_gather(pack(lo, hi)) for lo, hi in bounds]
        here = here_one = here_two = [packed] * 4
    else:
        here = chain(packed)
        across = others(here)
        pairs = [jnp.concatenate(pair, axis=0) for pair in zip(here, across)]
        pairs[-1] = jnp.concatenate([here[-1], across[-1], taps_rows], axis=0)
        pairs_y = [swap(pair, "tensor", 2) for pair in pairs]
        whole = jnp.concatenate(here + across + [taps_rows], axis=0)
        whole_y = jnp.concatenate(
            [pair[:block] for pair in pairs_y]
            + [pair[block : 2 * block] for pair in pairs_y]
            + [pairs_y[-1][2 * block :]],
            axis=0,
        )
        here_one = chain(pack(*bounds[0], here[deep // 2]))
        across_one = others(here_one)
        here_two = chain(pack(*bounds[1], here[-1], here_one[1]))
        across_two = others(here_two)
        blocks = [
            jnp.concatenate(here_one + across_one, axis=0),
            jnp.concatenate(here_two + across_two, axis=0),
        ]
    mix = [whole, swap(whole, "tensor", 1), whole_y, swap(whole_y, "tensor", 1)]

    lane = jnp.arange(width, dtype=jnp.int32)
    source = jnp.repeat(blocks_order()[0], block) * block + lane % block
    perm = (lane[:, None] == source[None, :]).astype(BF)
    perm_back = (source[:, None] == lane[None, :]).astype(BF)
    last = doc_ids.shape[0]
    ids = jnp.concatenate([doc_ids[:1], doc_ids[:1], doc_ids, doc_ids[last - 1 :], doc_ids[last - 1 :]])
    ids = lax.dynamic_slice(ids, (me_t * rows,), (rows + 4,))
    one_all = (ids[1:] == ids[:-1]).astype(F32)[:, None]
    two_all = (ids[2:] == ids[:-2]).astype(F32)[:, None]
    keep_one, keep_two = one_all[1 : rows + 1], two_all[:rows]
    next_one, next_two = one_all[2 : rows + 2], two_all[2 : rows + 2]
    cot = reorder(cotangent, perm)
    gains = reorder(jnp.stack([gain_mixer, gain_ffn]), perm).astype(F32)
    gain_one, gain_two = gains[:1], gains[1:]
    cot_y = swap(after(cot, whole_y), "tensor", 2)
    cot_c, cot_yc = swap(cot, "tensor", 1), swap(cot_y, "tensor", 1)
    extended = after(jnp.concatenate([halo, tokens_in], axis=0), here[1])
    extended = reorder(extended, perm)

    normed_ext, scale_ext = normalize(extended.astype(F32))
    hidden_ext = (normed_ext * gain_one).astype(BF)
    normed_one, scale_one = normed_ext[HALO:], scale_ext[HALO:]
    hidden_one = hidden_ext[HALO:]
    tokens_f = extended[HALO:].astype(F32)

    saved = []
    mixed = tokens_f
    earlier = [here_one[1], here_one[1], here_one[2], here_two[1]]
    for group, arrived in zip(mix, earlier):
        taps = group[width : width + 3, :channels].astype(F32)
        projected = nn(after(hidden_ext, arrived), group[:width, : 3 * channels])
        b_part = projected[:, :channels]
        v_part = projected[:, channels : 2 * channels]
        c_part = projected[HALO:, 2 * channels :]
        bx = b_part * v_part
        bx0, bx1, bx2 = bx[HALO:], keep_one * bx[HALO - 1 : -1], keep_two * bx[HALO - 2 : -2]
        conv_out = taps[0] * bx0 + taps[1] * bx1 + taps[2] * bx2
        gated = (c_part * conv_out).astype(BF)
        mixed = mixed + nt(gated, group[:width, 3 * channels :])
        saved.append((b_part[HALO:], c_part, v_part[HALO:], bx0, bx1, bx2, conv_out, gated, taps))
    resid = mixed
    normed_two, scale_two = normalize(resid)
    hidden_two = (normed_two * gain_two).astype(BF)
    hid_y = swap(hidden_two, "tensor", 2)
    hid_c, hid_yc = swap(hidden_two, "tensor", 1), swap(hid_y, "tensor", 1)
    hid = [jnp.concatenate([hidden_two, hid_c], axis=0), jnp.concatenate([hid_y, hid_yc], axis=0)]
    cots = [jnp.concatenate([cot, cot_c], axis=0), jnp.concatenate([cot_y, cot_yc], axis=0)]
    hid_all, cot_all = jnp.concatenate(hid, axis=0), jnp.concatenate(cots, axis=0)

    tile = min(rows, 256)

    def weight_grads(near, far, *earlier):
        d_gu, act = (jnp.concatenate([near[i], far[i]], axis=0) for i in (2, 3))
        tokens, grads = lax.optimization_barrier((hid_all, cot_all) + earlier)[:2]
        return [
            jnp.concatenate(
                [tn(tokens[:, part], d_gu).astype(BF), tn(grads[:, part], act).astype(BF)], axis=1
            )
            for part in (slice(half, width), slice(0, half))
        ]

    def over_x(parts):
        if long:
            return parts
        total = parts[1].astype(F32) + swap(parts[0], "dp", 1).astype(F32)
        return total.reshape(deep, block, -1)

    near = ffn(hid[0], cots[0], blocks[0], (), tile)
    far = ffn(hid[1], cots[1], blocks[0], (), tile)
    parts_one = weight_grads(near, far)
    sums_one = over_x(parts_one)
    far_two = ffn(after(hid[1], *parts_one), cots[1], blocks[1], tuple(far[:2]), tile)
    far_c = swap(far_two[0][rows:], "tensor", 1)
    near_two = ffn(after(hid[0], far_c), cots[0], blocks[1], tuple(near[:2]), tile)
    parts_two = weight_grads(near_two, far_two, near_two[0])
    sums_two = over_x(parts_two)

    d_far = far_two[0][:rows].astype(F32) + far_c.astype(F32)
    d_y = swap(d_far.astype(BF), "tensor", 2)
    d_hidden_two = near_two[0][:rows].astype(F32) + swap(near_two[0][rows:], "tensor", 1).astype(F32)
    d_hidden_two = d_hidden_two + d_y.astype(F32)
    d_hidden_two = after(d_hidden_two, sums_one[0], parts_two[1])
    out_far = far_two[1][:rows].astype(F32) + swap(far_two[1][rows:], "tensor", 1).astype(F32)
    out_y = swap(after(out_far.astype(BF), d_y), "tensor", 2)
    out_own = near_two[1][:rows].astype(F32) + swap(near_two[1][rows:], "tensor", 1).astype(F32)
    out_own = out_own + out_y.astype(F32)
    block_out = reorder((resid + out_own).astype(BF), perm_back)

    d_resid = cot.astype(F32) + norm_back(d_hidden_two * gain_two, normed_two, scale_two)
    d_mix = d_resid.astype(BF)

    d_gated = [nn(d_mix, group[:width, 3 * channels :]) for group in mix]
    d_conv = [back * keep[1] for back, keep in zip(d_gated, saved)]
    first = jnp.stack(by_xor([value[:2] for value in d_conv], me_t))
    following = shift(first, -1)
    following = by_xor([following[i] for i in range(4)], me_t)

    def step(run, sums, k):
        return ring(run.astype(BF), "dp", -2).astype(F32) + sums[k]

    run_one = sums_one if long else step(sums_one[deep - 1], sums_one, deep - 2)
    d_cs = [(d_gated[r] * saved[r][6]).astype(BF) for r in range(4)]
    right = [
        jnp.concatenate(
            [tn(hidden_one, d_cs[r]).astype(BF), tn(d_mix, saved[r][7]).astype(BF)], axis=1
        )
        for r in range(4)
    ]
    right_near = right[0].astype(F32) + swap(right[1], "tensor", 1).astype(F32)
    right_far = right[2].astype(F32) + swap(right[3], "tensor", 1).astype(F32)

    d_bvs = []
    for r in range(4):
        b_part, c_part, v_part, bx0, bx1, bx2, conv_out, gated, taps = saved[r]
        ahead = jnp.concatenate([d_conv[r], following[r]], axis=0)
        d_bx = (
            taps[0] * d_conv[r]
            + taps[1] * next_one * ahead[1 : rows + 1]
            + taps[2] * next_two * ahead[2:]
        )
        d_bvs.append(jnp.concatenate([d_bx * v_part, d_bx * b_part], axis=1).astype(BF))
    hidden_late = after(hidden_one, right[1], right[3], run_one[0])
    left = [tn(hidden_late, d_bvs[r]).astype(BF) for r in range(4)]
    left_near = left[0].astype(F32) + swap(left[1], "tensor", 1).astype(F32)
    left_far = left[2].astype(F32) + swap(left[3], "tensor", 1).astype(F32)
    if not long:
        run_one = step(run_one, sums_one, deep - 3)

    left_y = swap(after(left_far.astype(BF), out_y), "tensor", 2)
    left_sum = left_near + left_y.astype(F32)
    if long:
        right_sum = right_near + swap(right_far.astype(BF), "tensor", 2).astype(F32)
        total = jnp.concatenate([left_sum, right_sum], axis=1).astype(BF)
        mix_sum = long_scatter(total[:half], total[half:])
        ffn_grads = [long_scatter(parts[1], parts[0]) for parts in (sums_one, sums_two)]
        d_late = d_cs
    else:
        right_x = swap(jnp.concatenate([right_near[half:], right_far[half:]], axis=0).astype(BF), "dp", 1)
        right_near = right_near[:half] + right_x[:half].astype(F32)
        right_far = right_far[:half] + right_x[half:].astype(F32)
        right_sum = right_near + swap(right_far.astype(BF), "tensor", 2).astype(F32)
        left_sum = left_sum[:half] + swap(left_sum[half:].astype(BF), "dp", 1).astype(F32)

        def over_z(sums):
            sums = sums.reshape(deep, block, -1)
            low = sums.astype(BF)
            total = sums[0]
            for k in range(1, deep):
                total = total + ring(low[k], "dp", -2 * k).astype(F32)
            return total

        mix_sum = jnp.concatenate([over_z(left_sum), over_z(right_sum)], axis=1)
        for k in range(deep - 4, -1, -1):
            run_one = step(run_one, sums_one, k)
        run_two = sums_two[deep - 1]
        for k in range(deep - 2, -1, -1):
            run_two = step(run_two, sums_two, k)
        ffn_grads = [run_one, run_two]
        d_late = lax.optimization_barrier((d_cs, left[0], left[2], left[1], left[3]))[0]

    d_hidden_one = 0.0
    for r, group in enumerate(mix):
        d_proj = jnp.concatenate([d_bvs[r], d_late[r]], axis=1)
        d_hidden_one = d_hidden_one + nt(d_proj, group[:width, : 3 * channels])
    part_gain_one = jnp.sum(d_hidden_one * normed_one, axis=0)
    part_gain_two = jnp.sum(d_hidden_two * normed_two, axis=0)
    grad_input = d_resid + norm_back(d_hidden_one * gain_one, normed_one, scale_one)
    grad_input = reorder_f32(grad_input, perm_back)

    conv_parts = [
        jnp.stack([jnp.sum(value * d_conv[r], axis=0) for value in saved[r][3:6]]) for r in range(4)
    ]
    conv_all = jnp.stack(by_xor(conv_parts, me_t), axis=1)
    gain_parts = reorder_f32(jnp.stack([part_gain_one, part_gain_two]), perm_back)
    small = sum_all(jnp.concatenate([gain_parts, conv_all.reshape(-1, width)], axis=0))
    grad_conv = lax.dynamic_slice(small, (2, me_t * channels), (small.shape[0] - 2, channels))

    grad_in = jnp.stack([mix_sum[:, i * channels : (i + 1) * channels] for i in (0, 2, 1)], axis=1)
    grad_out = mix_sum[:, 3 * channels :].T
    grad_gu, grad_down = [], []
    for part, (lo, hi) in zip(ffn_grads, bounds):
        size = hi - lo
        grad_gu.append(part[:, : 2 * size].reshape(block, 2, size))
        grad_down.append(part[:, 2 * size :].T)
    return (
        block_out,
        grad_input,
        small[0],
        grad_in,
        grad_conv,
        grad_out,
        small[1],
        jnp.concatenate(grad_gu, axis=2),
        jnp.concatenate(grad_down, axis=0),
    )


def solution(mesh):
    return jax.shard_map(
        body,
        mesh=mesh,
        in_specs=(
            P(("dp", "tensor"), None),
            P("dp"),
            P(),
            P("dp", None, "tensor"),
            P(None, "tensor"),
            P("tensor", "dp"),
            P(),
            P("dp", None, "tensor"),
            P("tensor", "dp"),
            P(("dp", "tensor"), None),
        ),
        out_specs=(
            P(("dp", "tensor"), None),
            P(("dp", "tensor"), None),
            P(),
            P("dp", None, "tensor"),
            P(None, "tensor"),
            P("tensor", "dp"),
            P(),
            P("dp", None, "tensor"),
            P("tensor", "dp"),
        ),
        check_vma=False,
    )
```

```python
import jax
import jax.numpy as jnp
from jax import lax
from jax.experimental import pallas as pl
from jax.experimental.pallas import tpu as pltpu
from jax.sharding import PartitionSpec as P

epsilon = 1e-05
HALO = 16
LONG = 8
BF = jnp.bfloat16
F32 = jnp.float32


def swap(value, axis, bit):
    peers = lax.axis_size(axis)
    return lax.ppermute(value, axis, [(i, i ^ bit) for i in range(peers)])


def ring(value, axis, by):
    peers = lax.axis_size(axis)
    return lax.ppermute(value, axis, [(i, (i + by) % peers) for i in range(peers)])


def shift(value, by):
    peers = lax.axis_size("dp") * lax.axis_size("tensor")
    pairs = [(i, i + by) for i in range(peers) if 0 <= i + by < peers]
    return lax.ppermute(value, ("dp", "tensor"), pairs)


def nn(left, right):
    return jnp.dot(left, right, preferred_element_type=F32)


def tn(left, right):
    return lax.dot_general(left, right, (((0,), (0,)), ((), ())), preferred_element_type=F32)


def nt(left, right):
    return lax.dot_general(left, right, (((1,), (1,)), ((), ())), preferred_element_type=F32)


def normalize(values):
    scale_vec = lax.rsqrt(jnp.mean(values * values, axis=-1, keepdims=True) + epsilon)
    return (values * scale_vec, scale_vec)


def norm_back(d_normed, normed, scale_vec):
    return scale_vec * (d_normed - normed * jnp.mean(d_normed * normed, axis=-1, keepdims=True))


def after(value, *others):
    return lax.optimization_barrier((value,) + others)[0]


def reorder(values, perm):
    return nn(values, perm).astype(BF)


def reorder_f32(values, perm):
    high = lax.optimization_barrier(values.astype(BF))
    low = (values - high.astype(F32)).astype(BF)
    return nn(high, perm) + nn(low, perm)


def blocks_order():
    steps, me = lax.axis_size("dp") // 2, lax.axis_index("dp")
    index = jnp.arange(2 * steps, dtype=jnp.int32)
    order = ((me // 2 - index % steps) % steps) * 2 + ((me % 2) ^ (index // steps))
    inverse = ((index % 2) ^ (me % 2)) * steps + (me // 2 - index // 2) % steps
    return order, inverse


def long_gather(shard):
    whole = lax.all_gather(shard, "dp", axis=0)[blocks_order()[0]]
    return whole.reshape(-1, shard.shape[1])


def long_scatter(near, far):
    total = jnp.concatenate([near, far], axis=0)
    peers = lax.axis_size("dp")
    total = total.reshape(peers, total.shape[0] // peers, -1)[blocks_order()[1]].reshape(total.shape)
    return lax.psum_scatter(total, "dp", scatter_dimension=0, tiled=True).astype(F32)


def chain(shard):
    here = [shard]
    for _ in range(lax.axis_size("dp") // 2 - 1):
        here.append(ring(here[-1], "dp", 2))
    return here


def others(here):
    return [swap(piece, "dp", 1) for piece in here]


def ffn(hidden, cot, weights, order, before, kept, part, tile):
    rows, width = hidden.shape
    size = weights[0].shape[1] // 3
    count = order.shape[0]
    block = width // count
    skip = part * (rows // tile)

    def kernel(order_ref, h_ref, g_ref, *refs):
        w_any, refs = refs[: len(weights)], refs[len(weights) :]
        w_ref, sems = refs[-2:]
        d_ref, o_ref, d_gu_ref, act_ref = refs[-6:-2]

        @pl.when(pl.program_id(0) == 0)
        def _():
            if len(weights) > 1:
                pieces = w_any
            else:
                starts = [pl.multiple_of(order_ref[i] * block, block) for i in range(count)]
                pieces = [w_any[0].at[pl.ds(start, block)] for start in starts]
            copies = [
                pltpu.make_async_copy(piece, w_ref.at[pl.ds(i * block, block)], sems.at[i])
                for i, piece in enumerate(pieces)
            ]
            for copy in copies:
                copy.start()
            for copy in copies:
                copy.wait()

        gate_up = nn(h_ref[...], w_ref[:, : 2 * size])
        d_act = nn(g_ref[...], w_ref[:, 2 * size :])
        gate, up = gate_up[:, :size], gate_up[:, size:]
        sigma = 1.0 / (1.0 + jnp.exp(-gate))
        silu = gate * sigma
        act = (silu * up).astype(BF)
        act_ref[...] = act
        d_gu_ref[:, :size] = (d_act * up * (sigma * (1.0 + gate * (1.0 - sigma)))).astype(BF)
        d_gu_ref[:, size:] = (d_act * silu).astype(BF)
        d_sum = nt(d_gu_ref[...], w_ref[:, : 2 * size])
        o_sum = nt(act, w_ref[:, 2 * size :])
        if before:
            d_sum = d_sum + refs[0][...]
            o_sum = o_sum + refs[1][...]
        d_ref[...] = d_sum.astype(d_ref.dtype)
        o_ref[...] = o_sum.astype(o_ref.dtype)

    tokens = pl.BlockSpec((tile, width), lambda i, _: (i, 0))
    whole = pl.BlockSpec(memory_space=pl.ANY)
    kind = BF if before else F32
    aliased = 3 + len(weights) + len(before)
    return pl.pallas_call(
        kernel,
        grid_spec=pltpu.PrefetchScalarGridSpec(
            num_scalar_prefetch=1,
            grid=(rows // tile,),
            in_specs=[tokens] * 2 + [whole] * len(weights) + [tokens] * len(before) + [whole] * len(kept),
            out_specs=[
                tokens,
                tokens,
                pl.BlockSpec((tile, 2 * size), lambda i, _: (i + skip, 0)),
                pl.BlockSpec((tile, size), lambda i, _: (i + skip, 0)),
            ],
            scratch_shapes=[
                pltpu.VMEM((width, 3 * size), BF),
                pltpu.SemaphoreType.DMA((count,)),
            ],
        ),
        out_shape=[
            jax.ShapeDtypeStruct((rows, width), kind),
            jax.ShapeDtypeStruct((rows, width), kind),
            jax.ShapeDtypeStruct((2 * rows, 2 * size), BF),
            jax.ShapeDtypeStruct((2 * rows, size), BF),
        ],
        input_output_aliases={aliased: 2, aliased + 1: 3} if kept else {},
        compiler_params=pltpu.CompilerParams(vmem_limit_bytes=48 << 20),
        cost_estimate=pl.CostEstimate(
            flops=12 * rows * width * size,
            bytes_accessed=rows * width * 12 + width * size * 6,
            transcendentals=rows * size,
        ),
    )(order, hidden, cot, *weights, *before, *kept)


def by_xor(groups, me):
    one = [jnp.where((me & 1) == 1, groups[i ^ 1], groups[i]) for i in range(4)]
    return [jnp.where((me & 2) == 2, one[i ^ 2], one[i]) for i in range(4)]


def sum_all(value):
    return jnp.sum(lax.all_gather(value, ("dp", "tensor"), axis=0), axis=0)


def body(
    tokens_in,
    doc_ids,
    gain_mixer,
    in_weight,
    conv_weight,
    out_weight,
    gain_ffn,
    gate_up_weight,
    down_weight,
    cotangent,
):
    rows, width = tokens_in.shape
    dp_count = lax.axis_size("dp")
    block = width // dp_count
    channels = in_weight.shape[2]
    units = gate_up_weight.shape[2]
    me_t = lax.axis_index("tensor")
    deep = dp_count // 2
    half = width // 2
    long = deep > LONG

    tail = tokens_in[rows - HALO :]
    linked = (doc_ids[(me_t + 1) * rows - 2] == doc_ids[(me_t + 1) * rows - 1]).astype(BF)
    tail = tail * jnp.ones((HALO, 1), BF).at[HALO - 2, 0].set(linked)
    halo = shift(tail, 1)

    packed = jnp.concatenate(
        [in_weight[:, 0], in_weight[:, 2], in_weight[:, 1], out_weight.T], axis=1
    )
    taps_rows = jnp.zeros((HALO, 4 * channels), BF).at[:3, :channels].set(conv_weight)
    cut = units // 2 // 128 * 128
    bounds = [(0, cut), (cut, units)]

    shards = [
        jnp.concatenate(
            [gate_up_weight[:, 0, lo:hi], gate_up_weight[:, 1, lo:hi], down_weight[lo:hi].T], axis=1
        )
        for lo, hi in bounds
    ]
    block_two = [lax.all_gather(shards[1], "dp", axis=0, tiled=True)]

    if long:
        whole = jnp.concatenate([long_gather(packed), taps_rows], axis=0)
        whole_y = swap(whole, "tensor", 2)
        here = [packed] * 3
        block_one = [lax.all_gather(shards[0], "dp", axis=0, tiled=True)]
        here_one = across_one = block_one * 3
    else:
        here = chain(packed)
        across = others(here)
        pairs = [jnp.concatenate(pair, axis=0) for pair in zip(here, across)]
        pairs[-1] = jnp.concatenate([here[-1], across[-1], taps_rows], axis=0)
        pairs_y = [swap(pair, "tensor", 2) for pair in pairs]
        whole = jnp.concatenate(here + across + [taps_rows], axis=0)
        whole_y = jnp.concatenate(
            [pair[:block] for pair in pairs_y]
            + [pair[block : 2 * block] for pair in pairs_y]
            + [pairs_y[-1][2 * block :]],
            axis=0,
        )
        here_one = chain(after(shards[0], here[-1]))
        across_one = others(here_one)
        block_one = here_one + across_one
    mix = [whole, swap(whole, "tensor", 1), whole_y, swap(whole_y, "tensor", 1)]

    lane = jnp.arange(width, dtype=jnp.int32)
    order = blocks_order()[0]
    source = jnp.repeat(order, block) * block + lane % block
    perm = (lane[:, None] == source[None, :]).astype(BF)
    perm_back = (source[:, None] == lane[None, :]).astype(BF)
    doc_ids = after(doc_ids, here[2])
    last = doc_ids.shape[0]
    ids = jnp.concatenate([doc_ids[:1], doc_ids[:1], doc_ids, doc_ids[last - 1 :], doc_ids[last - 1 :]])
    ids = lax.dynamic_slice(ids, (me_t * rows,), (rows + 4,))
    one_all = (ids[1:] == ids[:-1]).astype(F32)[:, None]
    two_all = (ids[2:] == ids[:-2]).astype(F32)[:, None]
    keep_one, keep_two = one_all[1 : rows + 1], two_all[:rows]
    next_one, next_two = one_all[2 : rows + 2], two_all[2 : rows + 2]
    cot = reorder(after(cotangent, here[1]), perm)
    gains = reorder(jnp.stack([gain_mixer, gain_ffn]), perm).astype(F32)
    gain_one, gain_two = gains[:1], gains[1:]
    cot_y = swap(after(cot, whole_y), "tensor", 2)
    extended = after(jnp.concatenate([halo, tokens_in], axis=0), here[1])
    extended = reorder(extended, perm)

    normed_ext, scale_ext = normalize(extended.astype(F32))
    hidden_ext = (normed_ext * gain_one).astype(BF)
    normed_one, scale_one = normed_ext[HALO:], scale_ext[HALO:]
    hidden_one = hidden_ext[HALO:]
    tokens_f = extended[HALO:].astype(F32)

    saved = []
    mixed = tokens_f
    earlier = [(), (), (here_one[1],), (here_one[2], across_one[0])]
    for group, arrived in zip(mix, earlier):
        taps = group[width : width + 3, :channels].astype(F32)
        projected = nn(after(hidden_ext, *arrived), group[:width, : 3 * channels])
        b_part = projected[:, :channels]
        v_part = projected[:, channels : 2 * channels]
        c_part = projected[HALO:, 2 * channels :]
        bx = b_part * v_part
        bx0, bx1, bx2 = bx[HALO:], keep_one * bx[HALO - 1 : -1], keep_two * bx[HALO - 2 : -2]
        conv_out = taps[0] * bx0 + taps[1] * bx1 + taps[2] * bx2
        gated = (c_part * conv_out).astype(BF)
        mixed = mixed + nt(gated, group[:width, 3 * channels :])
        saved.append((b_part[HALO:], c_part, v_part[HALO:], bx0, bx1, bx2, conv_out, gated, taps))
    resid = mixed
    normed_two, scale_two = normalize(resid)
    hidden_two = (normed_two * gain_two).astype(BF)
    hid_y = swap(hidden_two, "tensor", 2)
    tile = min(rows, 256)

    def weight_grads(d_gu, act, earlier):
        parts = []
        for part, first in zip((slice(half, width), slice(0, half)), earlier):
            tokens, grads = lax.optimization_barrier((hid_all, cot_all) + first)[:2]
            grads = [tn(tokens[:, part], d_gu).astype(BF), tn(grads[:, part], act).astype(BF)]
            parts.append(jnp.concatenate(grads, axis=1))
        return parts

    def over_x(parts):
        if long:
            return parts
        total = parts[1].astype(F32) + swap(parts[0], "dp", 1).astype(F32)
        return total.reshape(deep, block, -1)

    hid = [jnp.concatenate([hidden_two, swap(hidden_two, "tensor", 1)], axis=0)]
    cots = [jnp.concatenate([cot, swap(cot, "tensor", 1)], axis=0)]
    near = ffn(after(hid[0], *block_two), cots[0], block_one, order, (), (), 0, tile)
    hid_y, cot_y = lax.optimization_barrier((hid_y, cot_y, near[0]))[:2]
    hid.append(jnp.concatenate([hid_y, swap(hid_y, "tensor", 1)], axis=0))
    cots.append(jnp.concatenate([cot_y, swap(cot_y, "tensor", 1)], axis=0))
    hid_all, cot_all = jnp.concatenate(hid, axis=0), jnp.concatenate(cots, axis=0)
    far = ffn(hid[1], cots[1], block_one, order, (), tuple(near[2:]), 1, tile)
    parts_one = weight_grads(*far[2:], ((), ()))
    sums_one = over_x(parts_one)
    far_two = ffn(after(hid[1], *parts_one), cots[1], block_two, order, tuple(far[:2]), (), 1, tile)
    d_far = far_two[0][:rows].astype(F32) + swap(far_two[0][rows:], "tensor", 1).astype(F32)
    d_far = d_far.astype(BF)
    d_y = [swap(part, "tensor", 2) for part in (d_far[: rows // 2], d_far[rows // 2 :])]
    near_two = ffn(
        after(hid[0], d_far), cots[0], block_two, order, tuple(near[:2]), tuple(far_two[2:]), 0, tile
    )
    parts_two = weight_grads(*near_two[2:], ((d_y[0],), ()))
    sums_two = over_x(parts_two)

    d_hidden_two = near_two[0][:rows].astype(F32) + swap(near_two[0][rows:], "tensor", 1).astype(F32)
    d_hidden_two = d_hidden_two + jnp.concatenate(d_y, axis=0).astype(F32)
    d_hidden_two = after(d_hidden_two, parts_two[1])
    out_far = far_two[1][:rows].astype(F32) + swap(far_two[1][rows:], "tensor", 1).astype(F32)
    out_y = swap(after(out_far.astype(BF), *d_y), "tensor", 2)
    out_own = near_two[1][:rows].astype(F32) + swap(near_two[1][rows:], "tensor", 1).astype(F32)
    out_own = out_own + out_y.astype(F32)
    block_out = reorder((resid + out_own).astype(BF), perm_back)

    d_resid = cot.astype(F32) + norm_back(d_hidden_two * gain_two, normed_two, scale_two)
    d_mix = d_resid.astype(BF)

    d_gated = [nn(d_mix, group[:width, 3 * channels :]) for group in mix]
    d_conv = [back * keep[1] for back, keep in zip(d_gated, saved)]
    first = jnp.stack(by_xor([value[:2] for value in d_conv], me_t))
    following = shift(first, -1)
    following = by_xor([following[i] for i in range(4)], me_t)

    def over_z(sums):
        sums = sums.reshape(deep, block, -1)
        low = sums.astype(BF)
        total = sums[0]
        for k in range(1, deep):
            total = total + ring(low[k], "dp", -2 * k).astype(F32)
        return total

    d_cs = [(d_gated[r] * saved[r][6]).astype(BF) for r in range(4)]
    right = [
        jnp.concatenate(
            [tn(hidden_one, d_cs[r]).astype(BF), tn(d_mix, saved[r][7]).astype(BF)], axis=1
        )
        for r in range(4)
    ]
    right_near = right[0].astype(F32) + swap(right[1], "tensor", 1).astype(F32)
    right_far = right[2].astype(F32) + swap(right[3], "tensor", 1).astype(F32)

    d_bvs = []
    for r in range(4):
        b_part, c_part, v_part, bx0, bx1, bx2, conv_out, gated, taps = saved[r]
        ahead = jnp.concatenate([d_conv[r], following[r]], axis=0)
        d_bx = (
            taps[0] * d_conv[r]
            + taps[1] * next_one * ahead[1 : rows + 1]
            + taps[2] * next_two * ahead[2:]
        )
        d_bvs.append(jnp.concatenate([d_bx * v_part, d_bx * b_part], axis=1).astype(BF))
    hidden_late = after(hidden_one, right[1], right[3], sums_one[0], out_y)
    left = [tn(hidden_late, d_bvs[r]).astype(BF) for r in range(4)]
    left_near = left[0].astype(F32) + swap(left[1], "tensor", 1).astype(F32)
    left_far = left[2].astype(F32) + swap(left[3], "tensor", 1).astype(F32)

    left_y = swap(left_far.astype(BF), "tensor", 2)
    left_sum = left_near + left_y.astype(F32)
    if long:
        right_sum = right_near + swap(right_far.astype(BF), "tensor", 2).astype(F32)
        total = jnp.concatenate([left_sum, right_sum], axis=1).astype(BF)
        mix_sum = long_scatter(total[:half], total[half:])
        ffn_grads = [long_scatter(parts[1], parts[0]) for parts in (sums_one, sums_two)]
        d_late = d_cs
    else:
        right_x = swap(jnp.concatenate([right_near[half:], right_far[half:]], axis=0).astype(BF), "dp", 1)
        right_near = right_near[:half] + right_x[:half].astype(F32)
        right_far = right_far[:half] + right_x[half:].astype(F32)
        right_sum = right_near + swap(right_far.astype(BF), "tensor", 2).astype(F32)
        left_sum = left_sum[:half] + swap(left_sum[half:].astype(BF), "dp", 1).astype(F32)

        mix_sum = jnp.concatenate([over_z(left_sum), over_z(right_sum)], axis=1)
        ffn_grads = [over_z(sums_one), over_z(sums_two)]
        d_late = lax.optimization_barrier((d_cs, left[0], left[2], left[1], left[3]))[0]

    d_hidden_one = 0.0
    for r, group in enumerate(mix):
        d_proj = jnp.concatenate([d_bvs[r], d_late[r]], axis=1)
        d_hidden_one = d_hidden_one + nt(d_proj, group[:width, : 3 * channels])
    part_gain_one = jnp.sum(d_hidden_one * normed_one, axis=0)
    part_gain_two = jnp.sum(d_hidden_two * normed_two, axis=0)
    grad_input = d_resid + norm_back(d_hidden_one * gain_one, normed_one, scale_one)
    grad_input = reorder_f32(grad_input, perm_back)

    conv_parts = [
        jnp.stack([jnp.sum(value * d_conv[r], axis=0) for value in saved[r][3:6]]) for r in range(4)
    ]
    conv_all = jnp.stack(by_xor(conv_parts, me_t), axis=1)
    gain_parts = reorder_f32(jnp.stack([part_gain_one, part_gain_two]), perm_back)
    small = sum_all(jnp.concatenate([gain_parts, conv_all.reshape(-1, width)], axis=0))
    grad_conv = lax.dynamic_slice(small, (2, me_t * channels), (small.shape[0] - 2, channels))

    grad_in = jnp.stack([mix_sum[:, i * channels : (i + 1) * channels] for i in (0, 2, 1)], axis=1)
    grad_out = mix_sum[:, 3 * channels :].T
    grad_gu, grad_down = [], []
    for part, (lo, hi) in zip(ffn_grads, bounds):
        size = hi - lo
        grad_gu.append(part[:, : 2 * size].reshape(block, 2, size))
        grad_down.append(part[:, 2 * size :].T)
    return (
        block_out,
        grad_input,
        small[0],
        grad_in,
        grad_conv,
        grad_out,
        small[1],
        jnp.concatenate(grad_gu, axis=2),
        jnp.concatenate(grad_down, axis=0),
    )


def solution(mesh):
    return jax.shard_map(
        body,
        mesh=mesh,
        in_specs=(
            P(("dp", "tensor"), None),
            P("dp"),
            P(),
            P("dp", None, "tensor"),
            P(None, "tensor"),
            P("tensor", "dp"),
            P(),
            P("dp", None, "tensor"),
            P("tensor", "dp"),
            P(("dp", "tensor"), None),
        ),
        out_specs=(
            P(("dp", "tensor"), None),
            P(("dp", "tensor"), None),
            P(),
            P("dp", None, "tensor"),
            P(None, "tensor"),
            P("tensor", "dp"),
            P(),
            P("dp", None, "tensor"),
            P("tensor", "dp"),
        ),
        check_vma=False,
    )
```

```python
import jax
import jax.numpy as jnp
from jax import lax
from jax.experimental import pallas as pl
from jax.experimental.pallas import tpu as pltpu
from jax.sharding import PartitionSpec as P

epsilon = 1e-05
HALO = 16
LONG = 8
BF = jnp.bfloat16
F32 = jnp.float32


def swap(value, axis, bit):
    peers = lax.axis_size(axis)
    return lax.ppermute(value, axis, [(i, i ^ bit) for i in range(peers)])


def ring(value, axis, by):
    peers = lax.axis_size(axis)
    return lax.ppermute(value, axis, [(i, (i + by) % peers) for i in range(peers)])


def shift(value, by):
    peers = lax.axis_size("dp") * lax.axis_size("tensor")
    pairs = [(i, i + by) for i in range(peers) if 0 <= i + by < peers]
    return lax.ppermute(value, ("dp", "tensor"), pairs)


def cross(value):
    inner = lax.axis_size("tensor")
    peers = lax.axis_size("dp") * inner
    return lax.ppermute(value, ("dp", "tensor"), [(i, i ^ (inner + 2)) for i in range(peers)])


def nn(left, right):
    return jnp.dot(left, right, preferred_element_type=F32)


def tn(left, right):
    return lax.dot_general(left, right, (((0,), (0,)), ((), ())), preferred_element_type=F32)


def nt(left, right):
    return lax.dot_general(left, right, (((1,), (1,)), ((), ())), preferred_element_type=F32)


def normalize(values):
    scale_vec = lax.rsqrt(jnp.mean(values * values, axis=-1, keepdims=True) + epsilon)
    return (values * scale_vec, scale_vec)


def norm_back(d_normed, normed, scale_vec):
    return scale_vec * (d_normed - normed * jnp.mean(d_normed * normed, axis=-1, keepdims=True))


def after(value, *others):
    return lax.optimization_barrier((value,) + others)[0]


def reorder(values, perm):
    return nn(values, perm).astype(BF)


def reorder_f32(values, perm):
    high = lax.optimization_barrier(values.astype(BF))
    low = (values - high.astype(F32)).astype(BF)
    return nn(high, perm) + nn(low, perm)


def blocks_order():
    steps, me = lax.axis_size("dp") // 2, lax.axis_index("dp")
    index = jnp.arange(2 * steps, dtype=jnp.int32)
    order = ((me // 2 - index % steps) % steps) * 2 + ((me % 2) ^ (index // steps))
    inverse = ((index % 2) ^ (me % 2)) * steps + (me // 2 - index // 2) % steps
    return order, inverse


def long_gather(shard):
    whole = lax.all_gather(shard, "dp", axis=0)[blocks_order()[0]]
    return whole.reshape(-1, shard.shape[1])


def long_scatter(near, far):
    total = jnp.concatenate([near, far], axis=0)
    peers = lax.axis_size("dp")
    total = total.reshape(peers, total.shape[0] // peers, -1)[blocks_order()[1]].reshape(total.shape)
    return lax.psum_scatter(total, "dp", scatter_dimension=0, tiled=True).astype(F32)


def chain(shard):
    here = [shard]
    for _ in range(lax.axis_size("dp") // 2 - 1):
        here.append(ring(here[-1], "dp", 2))
    return here


def others(here):
    return [swap(piece, "dp", 1) for piece in here]


def ffn(hidden, cot, weights, order, before, kept, part, tile):
    rows, width = 2 * hidden[0].shape[0], hidden[0].shape[1]
    size = weights[0].shape[1] // 3
    count = order.shape[0]
    block = width // count
    steps = rows // tile
    skip = part * steps

    def kernel(order_ref, *refs):
        slots, w_any, refs = refs[:4], refs[4 : 4 + len(weights)], refs[4 + len(weights) :]
        w_ref, sems, h_ref, g_ref = refs[-4:]
        sum_ref, d_gu_ref, act_ref = refs[-7:-4]

        @pl.when(pl.program_id(0) == 0)
        def _():
            if len(weights) > 1:
                pieces = w_any
            else:
                starts = [pl.multiple_of(order_ref[i] * block, block) for i in range(count)]
                pieces = [w_any[0].at[pl.ds(start, block)] for start in starts]
            copies = [
                pltpu.make_async_copy(piece, w_ref.at[pl.ds(i * block, block)], sems.at[i])
                for i, piece in enumerate(pieces)
            ]
            for copy in copies:
                copy.start()
            for copy in copies:
                copy.wait()

        for slot in (0, 1):

            @pl.when(pl.program_id(0) // (steps // 2) == slot)
            def _(slot=slot):
                h_ref[...] = slots[slot][...]
                g_ref[...] = slots[2 + slot][...]

        gate_up = nn(h_ref[...], w_ref[:, : 2 * size])
        d_act = nn(g_ref[...], w_ref[:, 2 * size :])
        gate, up = gate_up[:, :size], gate_up[:, size:]
        sigma = 1.0 / (1.0 + jnp.exp(-gate))
        silu = gate * sigma
        act = (silu * up).astype(BF)
        act_ref[...] = act
        d_gu_ref[:, :size] = (d_act * up * (sigma * (1.0 + gate * (1.0 - sigma)))).astype(BF)
        d_gu_ref[:, size:] = (d_act * silu).astype(BF)
        d_sum = nt(d_gu_ref[...], w_ref[:, : 2 * size])
        o_sum = nt(act, w_ref[:, 2 * size :])
        if before:
            d_sum = d_sum + refs[0][:, :width]
            o_sum = o_sum + refs[0][:, width:]
        sum_ref[:, :width] = d_sum.astype(sum_ref.dtype)
        sum_ref[:, width:] = o_sum.astype(sum_ref.dtype)

    tokens = pl.BlockSpec((tile, 2 * width), lambda i, _: (i, 0))
    whole = pl.BlockSpec(memory_space=pl.ANY)
    near = pl.BlockSpec((tile, width), lambda i, _: (jnp.minimum(i, steps // 2 - 1), 0))
    far = pl.BlockSpec((tile, width), lambda i, _: (jnp.maximum(i - steps // 2, 0), 0))
    kind = BF if before else F32
    aliased = 5 + len(weights) + len(before)
    return pl.pallas_call(
        kernel,
        grid_spec=pltpu.PrefetchScalarGridSpec(
            num_scalar_prefetch=1,
            grid=(rows // tile,),
            in_specs=[near, far] * 2 + [whole] * len(weights) + [tokens] * len(before) + [whole] * len(kept),
            out_specs=[
                tokens,
                pl.BlockSpec((tile, 2 * size), lambda i, _: (i + skip, 0)),
                pl.BlockSpec((tile, size), lambda i, _: (i + skip, 0)),
            ],
            scratch_shapes=[
                pltpu.VMEM((width, 3 * size), BF),
                pltpu.SemaphoreType.DMA((count,)),
                pltpu.VMEM((tile, width), BF),
                pltpu.VMEM((tile, width), BF),
            ],
        ),
        out_shape=[
            jax.ShapeDtypeStruct((rows, 2 * width), kind),
            jax.ShapeDtypeStruct((2 * rows, 2 * size), BF),
            jax.ShapeDtypeStruct((2 * rows, size), BF),
        ],
        input_output_aliases={aliased: 1, aliased + 1: 2} if kept else {},
        compiler_params=pltpu.CompilerParams(vmem_limit_bytes=48 << 20),
        cost_estimate=pl.CostEstimate(
            flops=12 * rows * width * size,
            bytes_accessed=rows * width * 12 + width * size * 6,
            transcendentals=rows * size,
        ),
    )(order, *hidden, *cot, *weights, *before, *kept)


def by_xor(groups, me):
    one = [jnp.where((me & 1) == 1, groups[i ^ 1], groups[i]) for i in range(4)]
    return [jnp.where((me & 2) == 2, one[i ^ 2], one[i]) for i in range(4)]


def body(
    tokens_in,
    doc_ids,
    gain_mixer,
    in_weight,
    conv_weight,
    out_weight,
    gain_ffn,
    gate_up_weight,
    down_weight,
    cotangent,
):
    rows, width = tokens_in.shape
    dp_count = lax.axis_size("dp")
    block = width // dp_count
    channels = in_weight.shape[2]
    units = gate_up_weight.shape[2]
    me_t = lax.axis_index("tensor")
    deep = dp_count // 2
    half = width // 2
    long = deep > LONG

    tail = tokens_in[rows - HALO :]
    linked = (doc_ids[(me_t + 1) * rows - 2] == doc_ids[(me_t + 1) * rows - 1]).astype(BF)
    tail = tail * jnp.ones((HALO, 1), BF).at[HALO - 2, 0].set(linked)
    halo = shift(tail, 1)

    packed = jnp.concatenate(
        [in_weight[:, 0], in_weight[:, 2], in_weight[:, 1], out_weight.T], axis=1
    )
    taps_rows = jnp.zeros((HALO, 4 * channels), BF).at[:3, :channels].set(conv_weight)
    cut = units // 2 // 128 * 128
    bounds = [(0, cut), (cut, units)]

    shards = [
        jnp.concatenate(
            [gate_up_weight[:, 0, lo:hi], gate_up_weight[:, 1, lo:hi], down_weight[lo:hi].T], axis=1
        )
        for lo, hi in bounds
    ]

    if long:
        whole = jnp.concatenate([long_gather(packed), taps_rows], axis=0)
        whole_y = swap(whole, "tensor", 2)
        here = [packed] * 3
        block_one = [lax.all_gather(shards[0], "dp", axis=0, tiled=True)]
        here_one = across_one = block_one * 3
    else:
        here = chain(packed)
        across = others(here)
        pairs = [jnp.concatenate(pair, axis=0) for pair in zip(here, across)]
        pairs[-1] = jnp.concatenate([here[-1], across[-1], taps_rows], axis=0)
        pairs_y = [swap(pair, "tensor", 2) for pair in pairs]
        whole = jnp.concatenate(here + across + [taps_rows], axis=0)
        whole_y = jnp.concatenate(
            [pair[:block] for pair in pairs_y]
            + [pair[block : 2 * block] for pair in pairs_y]
            + [pairs_y[-1][2 * block :]],
            axis=0,
        )
        here_one = chain(after(shards[0], here[-1]))
        across_one = others(here_one)
        block_one = here_one + across_one
    block_two = [lax.all_gather(after(shards[1], here[-1]), "dp", axis=0, tiled=True)]
    mix = [whole, swap(whole, "tensor", 1), whole_y, swap(whole_y, "tensor", 1)]

    lane = jnp.arange(width, dtype=jnp.int32)
    order = blocks_order()[0]
    source = jnp.repeat(order, block) * block + lane % block
    perm = (lane[:, None] == source[None, :]).astype(BF)
    perm_back = (source[:, None] == lane[None, :]).astype(BF)
    doc_ids = after(doc_ids, here[2])
    last = doc_ids.shape[0]
    ids = jnp.concatenate([doc_ids[:1], doc_ids[:1], doc_ids, doc_ids[last - 1 :], doc_ids[last - 1 :]])
    ids = lax.dynamic_slice(ids, (me_t * rows,), (rows + 4,))
    one_all = (ids[1:] == ids[:-1]).astype(F32)[:, None]
    two_all = (ids[2:] == ids[:-2]).astype(F32)[:, None]
    keep_one, keep_two = one_all[1 : rows + 1], two_all[:rows]
    next_one, next_two = one_all[2 : rows + 2], two_all[2 : rows + 2]
    cot = reorder(after(cotangent, here[1]), perm)
    gains = reorder(jnp.stack([gain_mixer, gain_ffn]), perm).astype(F32)
    gain_one, gain_two = gains[:1], gains[1:]
    cot_y = swap(after(cot, whole_y), "tensor", 2)
    extended = after(jnp.concatenate([halo, tokens_in], axis=0), here[1])
    extended = reorder(extended, perm)

    normed_ext, scale_ext = normalize(extended.astype(F32))
    hidden_ext = (normed_ext * gain_one).astype(BF)
    normed_one, scale_one = normed_ext[HALO:], scale_ext[HALO:]
    hidden_one = hidden_ext[HALO:]
    tokens_f = extended[HALO:].astype(F32)

    saved = []
    mixed = tokens_f
    earlier = [(), (), (here_one[1],), (here_one[2], across_one[0])]
    for group, arrived in zip(mix, earlier):
        taps = group[width : width + 3, :channels].astype(F32)
        projected = nn(after(hidden_ext, *arrived), group[:width, : 3 * channels])
        b_part = projected[:, :channels]
        v_part = projected[:, channels : 2 * channels]
        c_part = projected[HALO:, 2 * channels :]
        bx = b_part * v_part
        bx0, bx1, bx2 = bx[HALO:], keep_one * bx[HALO - 1 : -1], keep_two * bx[HALO - 2 : -2]
        conv_out = taps[0] * bx0 + taps[1] * bx1 + taps[2] * bx2
        gated = (c_part * conv_out).astype(BF)
        mixed = mixed + nt(gated, group[:width, 3 * channels :])
        saved.append((b_part[HALO:], c_part, v_part[HALO:], bx0, bx1, bx2, conv_out, gated, taps))
    resid = mixed
    normed_two, scale_two = normalize(resid)
    hidden_two = (normed_two * gain_two).astype(BF)
    hid_y = swap(hidden_two, "tensor", 2)
    tile = min(rows // 2, 256)

    def weight_grads(d_gu, act, earlier):
        parts = []
        for part, first in zip((slice(half, width), slice(0, half)), earlier):
            tokens, grads = lax.optimization_barrier((hid_all, cot_all) + first)[:2]
            grads = [tn(tokens[:, part], d_gu).astype(BF), tn(grads[:, part], act).astype(BF)]
            parts.append(jnp.concatenate(grads, axis=1))
        return parts

    def over_x(parts, *late):
        if long:
            return parts
        total = parts[1].astype(F32) + after(swap(parts[0], "dp", 1), *late).astype(F32)
        return total.reshape(deep, block, -1)

    hid = [[hidden_two, swap(hidden_two, "tensor", 1)]]
    cots = [[cot, swap(cot, "tensor", 1)]]
    hid[0][0] = after(hid[0][0], *block_two)
    near = ffn(hid[0], cots[0], block_one, order, (), (), 0, tile)
    hid_y, cot_y = lax.optimization_barrier((hid_y, cot_y, near[0]))[:2]
    hid.append([hid_y, swap(hid_y, "tensor", 1)])
    cots.append([cot_y, swap(cot_y, "tensor", 1)])
    far = ffn(hid[1], cots[1], block_one, order, (), tuple(near[1:]), 1, tile)
    hid_all, cot_all = jnp.concatenate(hid[0] + hid[1], axis=0), jnp.concatenate(cots[0] + cots[1], axis=0)
    parts_one = weight_grads(*far[1:], ((), ()))
    far_two = ffn(
        [after(hid[1][0], *parts_one), hid[1][1]], cots[1], block_two, order, (far[0],), (), 1, tile
    )

    far_core = swap(far_two[0][rows:], "tensor", 1)
    sum_far = (far_two[0][:rows].astype(F32) + far_core.astype(F32)).astype(BF)
    d_far, out_far = sum_far[:, :width], sum_far[:, width:]
    d_y = [swap(part, "tensor", 2) for part in (d_far[: rows // 2], d_far[rows // 2 :])]
    near_two = ffn(
        [after(hid[0][0], far_core), hid[0][1]], cots[0], block_two, order, (near[0],), tuple(far_two[1:]), 0, tile
    )
    parts_two = weight_grads(*near_two[1:], ((d_y[0],), ()))
    sums_one, sums_two = over_x(parts_one, near_two[1]), over_x(parts_two)

    near_core = swap(near_two[0][rows:], "tensor", 1)
    sum_near = near_two[0][:rows].astype(F32) + near_core.astype(F32)
    d_hidden_two = sum_near[:, :width] + jnp.concatenate(d_y, axis=0).astype(F32)
    d_hidden_two = after(d_hidden_two, parts_two[1])
    out_y = swap(after(out_far, *d_y), "tensor", 2)
    out_own = sum_near[:, width:] + out_y.astype(F32)
    block_out = reorder((resid + out_own).astype(BF), perm_back)

    d_resid = cot.astype(F32) + norm_back(d_hidden_two * gain_two, normed_two, scale_two)
    d_mix = d_resid.astype(BF)

    d_gated = [nn(d_mix, group[:width, 3 * channels :]) for group in mix]
    d_conv = [back * keep[1] for back, keep in zip(d_gated, saved)]
    first = jnp.stack(by_xor([value[:2] for value in d_conv], me_t))
    following = shift(first, -1)
    following = by_xor([following[i] for i in range(4)], me_t)

    def add_z(sums):
        return sum(
            [sums[0]] + [ring(sums[k].astype(BF), "dp", -2 * k).astype(F32) for k in range(1, deep)]
        )

    def fold(sums, late):
        if long:
            return sums, late
        part = sums.shape[0] // 2
        got = ring(sums[part:].astype(BF), "dp", -2 * part)
        got, late = lax.optimization_barrier((got, late))
        return sums[:part] + got.astype(F32), late

    sums_one, d_conv[0] = fold(sums_one, d_conv[0])
    d_cs = [(d_gated[r] * saved[r][6]).astype(BF) for r in range(4)]

    def sides(values, r):
        return jnp.concatenate([values[r], values[r + 2]], axis=1)

    gates = [saved[r][7] for r in range(4)]
    right = [
        jnp.concatenate(
            [tn(hidden_one, sides(d_cs, r)).astype(BF), tn(d_mix, sides(gates, r)).astype(BF)], axis=1
        )
        for r in (1, 0)
    ]
    right_core = swap(right[0], "tensor", 1)

    d_bvs = []
    for r in range(4):
        b_part, c_part, v_part, bx0, bx1, bx2, conv_out, gated, taps = saved[r]
        ahead = jnp.concatenate([d_conv[r], following[r]], axis=0)
        d_bx = (
            taps[0] * d_conv[r]
            + taps[1] * next_one * ahead[1 : rows + 1]
            + taps[2] * next_two * ahead[2:]
        )
        d_bvs.append(jnp.concatenate([d_bx * v_part, d_bx * b_part], axis=1).astype(BF))
    sums_one, hidden_late = fold(sums_one, after(hidden_one, *right, sums_two, out_y))
    left = [tn(hidden_late, sides(d_bvs, r)).astype(BF) for r in (1, 0)]
    left_core = swap(left[0], "tensor", 1)

    side = 2 * channels
    right_all = right[1].astype(F32) + right_core.astype(F32)
    right_near, right_far = (
        jnp.concatenate([right_all[:, i : i + channels], right_all[:, i + side : i + side + channels]], axis=1)
        for i in (0, channels)
    )
    left_all = left[1].astype(F32) + left_core.astype(F32)
    left_near, left_far = left_all[:, :side], left_all[:, side:]
    left_y = swap(left_far.astype(BF), "tensor", 2)
    left_sum = left_near + left_y.astype(F32)
    if long:
        right_sum = right_near + swap(right_far.astype(BF), "tensor", 2).astype(F32)
        total = jnp.concatenate([left_sum, right_sum], axis=1).astype(BF)
        mix_sum = long_scatter(total[:half], total[half:])
        ffn_grads = [long_scatter(parts[1], parts[0]) for parts in (sums_one, sums_two)]
        d_late = d_cs
    else:
        right_x = swap(jnp.concatenate([right_near[half:], right_far[half:]], axis=0).astype(BF), "dp", 1)
        right_near = right_near[:half] + right_x[:half].astype(F32)
        right_far = right_far[:half] + right_x[half:].astype(F32)
        sums_two, right_far = fold(sums_two, right_far)
        right_sum = right_near + swap(right_far.astype(BF), "tensor", 2).astype(F32)
        left_sum = left_sum[:half] + swap(left_sum[half:].astype(BF), "dp", 1).astype(F32)
        total = jnp.concatenate([left_sum, right_sum], axis=1).reshape(deep, block, -1)
        sums_two, total = fold(sums_two, total)
        mix_sum = add_z(total)
        ffn_grads = [sums_one[0], sums_two[0]]
        d_late = lax.optimization_barrier((d_cs, *left))[0]

    d_hidden_one = 0.0
    for r, group in enumerate(mix):
        d_proj = jnp.concatenate([d_bvs[r], d_late[r]], axis=1)
        d_hidden_one = d_hidden_one + nt(d_proj, group[:width, : 3 * channels])
    part_gain_one = jnp.sum(d_hidden_one * normed_one, axis=0)
    part_gain_two = jnp.sum(d_hidden_two * normed_two, axis=0)
    grad_input = d_resid + norm_back(d_hidden_one * gain_one, normed_one, scale_one)
    grad_input = reorder_f32(grad_input, perm_back)

    conv_parts = [
        jnp.stack([jnp.sum(value * d_conv[r], axis=0) for value in saved[r][3:6]]) for r in range(4)
    ]
    conv_all = jnp.stack(by_xor(conv_parts, me_t), axis=1)
    gain_parts = reorder_f32(jnp.stack([part_gain_one, part_gain_two]), perm_back)
    small = jnp.concatenate([gain_parts, conv_all.reshape(-1, width)], axis=0)
    if long:
        small = lax.psum(small, ("dp", "tensor"))
    else:
        small = small + swap(small, "tensor", 1)
        bit = deep // 2
        while bit:
            small = small + ring(small, "dp", 2 * bit)
            bit //= 2
        small = after(small, right_x)
        got = [swap(small, "dp", 1), swap(small, "tensor", 2), cross(small)]
        small = sum(lax.optimization_barrier((small, *got, total))[:4])
    grad_conv = lax.dynamic_slice(small, (2, me_t * channels), (small.shape[0] - 2, channels))

    grad_in = jnp.stack([mix_sum[:, i * channels : (i + 1) * channels] for i in (0, 2, 1)], axis=1)
    grad_out = mix_sum[:, 3 * channels :].T
    grad_gu, grad_down = [], []
    for part, (lo, hi) in zip(ffn_grads, bounds):
        size = hi - lo
        grad_gu.append(part[:, : 2 * size].reshape(block, 2, size))
        grad_down.append(part[:, 2 * size :].T)
    return (
        block_out,
        grad_input,
        small[0],
        grad_in,
        grad_conv,
        grad_out,
        small[1],
        jnp.concatenate(grad_gu, axis=2),
        jnp.concatenate(grad_down, axis=0),
    )


def solution(mesh):
    return jax.shard_map(
        body,
        mesh=mesh,
        in_specs=(
            P(("dp", "tensor"), None),
            P("dp"),
            P(),
            P("dp", None, "tensor"),
            P(None, "tensor"),
            P("tensor", "dp"),
            P(),
            P("dp", None, "tensor"),
            P("tensor", "dp"),
            P(("dp", "tensor"), None),
        ),
        out_specs=(
            P(("dp", "tensor"), None),
            P(("dp", "tensor"), None),
            P(),
            P("dp", None, "tensor"),
            P(None, "tensor"),
            P("tensor", "dp"),
            P(),
            P("dp", None, "tensor"),
            P("tensor", "dp"),
        ),
        check_vma=False,
    )
```

```python
import jax
import jax.numpy as jnp
from jax import lax
from jax.experimental import pallas as pl
from jax.experimental.pallas import tpu as pltpu
from jax.sharding import PartitionSpec as P

epsilon = 1e-05
HALO = 16
LONG = 8
BF = jnp.bfloat16
F32 = jnp.float32


def swap(value, axis, bit):
    peers = lax.axis_size(axis)
    return lax.ppermute(value, axis, [(i, i ^ bit) for i in range(peers)])


def ring(value, axis, by):
    peers = lax.axis_size(axis)
    return lax.ppermute(value, axis, [(i, (i + by) % peers) for i in range(peers)])


def shift(value, by):
    peers = lax.axis_size("dp") * lax.axis_size("tensor")
    pairs = [(i, i + by) for i in range(peers) if 0 <= i + by < peers]
    return lax.ppermute(value, ("dp", "tensor"), pairs)


def cross(value):
    inner = lax.axis_size("tensor")
    peers = lax.axis_size("dp") * inner
    return lax.ppermute(value, ("dp", "tensor"), [(i, i ^ (inner + 2)) for i in range(peers)])


def nn(left, right):
    return jnp.dot(left, right, preferred_element_type=F32)


def tn(left, right):
    return lax.dot_general(left, right, (((0,), (0,)), ((), ())), preferred_element_type=F32)


def nt(left, right):
    return lax.dot_general(left, right, (((1,), (1,)), ((), ())), preferred_element_type=F32)


def normalize(values):
    scale_vec = lax.rsqrt(jnp.mean(values * values, axis=-1, keepdims=True) + epsilon)
    return (values * scale_vec, scale_vec)


def norm_back(d_normed, normed, scale_vec):
    return scale_vec * (d_normed - normed * jnp.mean(d_normed * normed, axis=-1, keepdims=True))


def after(value, *others):
    return lax.optimization_barrier((value,) + others)[0]


def reorder(values, perm):
    return nn(values, perm).astype(BF)


def reorder_f32(values, perm):
    high = lax.optimization_barrier(values.astype(BF))
    low = (values - high.astype(F32)).astype(BF)
    return nn(high, perm) + nn(low, perm)


def blocks_order():
    steps, me = lax.axis_size("dp") // 2, lax.axis_index("dp")
    index = jnp.arange(2 * steps, dtype=jnp.int32)
    order = ((me // 2 - index % steps) % steps) * 2 + ((me % 2) ^ (index // steps))
    inverse = ((index % 2) ^ (me % 2)) * steps + (me // 2 - index // 2) % steps
    return order, inverse


def long_gather(shard):
    whole = lax.all_gather(shard, "dp", axis=0)[blocks_order()[0]]
    return whole.reshape(-1, shard.shape[1])


def long_scatter(near, far):
    total = jnp.concatenate([near, far], axis=0)
    peers = lax.axis_size("dp")
    total = total.reshape(peers, total.shape[0] // peers, -1)[blocks_order()[1]].reshape(total.shape)
    return lax.psum_scatter(total, "dp", scatter_dimension=0, tiled=True).astype(F32)


def chain(shard):
    here = [shard]
    for _ in range(lax.axis_size("dp") // 2 - 1):
        here.append(ring(here[-1], "dp", 2))
    return here


def others(here):
    return [swap(piece, "dp", 1) for piece in here]


def ffn(hidden, cot, weights, before, kept, part, tile):
    slot_rows, width = hidden[0].shape
    rows = 2 * slot_rows
    size = weights.shape[1] // 3
    steps = rows // tile
    skip = part * steps
    wide = [2 * size, size] + ([] if before else [width, width])

    def kernel(*refs):
        slots, w_ref, refs = refs[:4], refs[4], refs[5:]
        if before:
            h_ref, g_ref = refs[-2:]
            refs = refs[:-2]
        else:
            h_ref, g_ref = refs[-2:]
        outs = refs[len(before) + len(kept) :]
        d_gu_ref, act_ref = outs[4:6]

        def at(slot):
            return pl.when(pl.program_id(0) // (steps // 2) == slot)

        for slot in (0, 1):

            @at(slot)
            def _(slot=slot):
                h_ref[...] = slots[slot][...]
                g_ref[...] = slots[2 + slot][...]

        gate_up = nn(h_ref[...], w_ref[:, : 2 * size])
        d_act = nn(g_ref[...], w_ref[:, 2 * size :])
        gate, up = gate_up[:, :size], gate_up[:, size:]
        sigma = 1.0 / (1.0 + jnp.exp(-gate))
        silu = gate * sigma
        act = (silu * up).astype(BF)
        act_ref[...] = act
        d_gu_ref[:, :size] = (d_act * up * (sigma * (1.0 + gate * (1.0 - sigma)))).astype(BF)
        d_gu_ref[:, size:] = (d_act * silu).astype(BF)
        sums = [nt(d_gu_ref[...], w_ref[:, : 2 * size]), nt(act, w_ref[:, 2 * size :])]
        for slot in (0, 1):

            @at(slot)
            def _(slot=slot):
                for i, value in enumerate(sums):
                    at_ref = outs[2 * slot + i]
                    if before:
                        value = value + refs[2 * slot + i][...]
                    at_ref[...] = value.astype(at_ref.dtype)

    whole = pl.BlockSpec(memory_space=pl.ANY)
    near = pl.BlockSpec((tile, width), lambda i: (jnp.minimum(i, steps // 2 - 1), 0))
    far = pl.BlockSpec((tile, width), lambda i: (jnp.maximum(i - steps // 2, 0), 0))
    kind = BF if before else F32
    aliased = 5 + len(before)
    return pl.pallas_call(
        kernel,
        grid=(steps,),
        in_specs=[near, far] * 2
        + [pl.BlockSpec(weights.shape, lambda i: (0, 0))]
        + [near, near, far, far][: len(before)]
        + [whole] * len(kept),
        out_specs=[near, near, far, far] + [pl.BlockSpec((tile, n), lambda i: (i + skip, 0)) for n in wide],
        out_shape=[jax.ShapeDtypeStruct((slot_rows, width), kind)] * 4
        + [jax.ShapeDtypeStruct((2 * rows, n), BF) for n in wide],
        scratch_shapes=[pltpu.VMEM((tile, width), BF)] * (2 if before else 0),
        input_output_aliases={aliased + i: 4 + i for i in range(len(kept))},
        compiler_params=pltpu.CompilerParams(vmem_limit_bytes=48 << 20),
        cost_estimate=pl.CostEstimate(
            flops=12 * rows * width * size,
            bytes_accessed=rows * width * 12 + width * size * 6,
            transcendentals=rows * size,
        ),
    )(*hidden, *cot, weights, *before, *kept)


def by_xor(groups, me):
    one = [jnp.where((me & 1) == 1, groups[i ^ 1], groups[i]) for i in range(4)]
    return [jnp.where((me & 2) == 2, one[i ^ 2], one[i]) for i in range(4)]


def body(
    tokens_in,
    doc_ids,
    gain_mixer,
    in_weight,
    conv_weight,
    out_weight,
    gain_ffn,
    gate_up_weight,
    down_weight,
    cotangent,
):
    rows, width = tokens_in.shape
    dp_count = lax.axis_size("dp")
    block = width // dp_count
    channels = in_weight.shape[2]
    units = gate_up_weight.shape[2]
    me_t = lax.axis_index("tensor")
    deep = dp_count // 2
    half = width // 2
    long = deep > LONG

    tail = tokens_in[rows - HALO :]
    linked = (doc_ids[(me_t + 1) * rows - 2] == doc_ids[(me_t + 1) * rows - 1]).astype(BF)
    tail = tail * jnp.ones((HALO, 1), BF).at[HALO - 2, 0].set(linked)
    halo = shift(tail, 1)

    packed = jnp.concatenate(
        [in_weight[:, 0], in_weight[:, 2], in_weight[:, 1], out_weight.T], axis=1
    )
    taps_rows = jnp.zeros((HALO, 4 * channels), BF).at[:3, :channels].set(conv_weight)
    cut = units // 2 // 128 * 128
    bounds = [(0, cut), (cut, units)]


    def gather_block(lo, hi, *earlier):
        gate_up, down = lax.optimization_barrier((gate_up_weight, down_weight) + earlier)[:2]
        shard = jnp.concatenate([gate_up[:, 0, lo:hi], gate_up[:, 1, lo:hi], down[lo:hi].T], axis=1)
        return lax.all_gather(shard, "dp", axis=0, tiled=True)

    cot_y = swap(after(cotangent, halo), "tensor", 2)
    if long:
        whole = jnp.concatenate([long_gather(packed), taps_rows], axis=0)
        whole_y = swap(whole, "tensor", 2)
        here = [packed] * 3
    else:
        here = chain(packed)
        across = others(here)
        pairs = [jnp.concatenate(pair, axis=0) for pair in zip(here, across)]
        pairs[-1] = jnp.concatenate([here[-1], across[-1], taps_rows], axis=0)
        pairs[-1] = after(pairs[-1], cot_y)
        pairs_y = [swap(pair, "tensor", 2) for pair in pairs]
        whole = jnp.concatenate(here + across + [taps_rows], axis=0)
        whole_y = jnp.concatenate(
            [pair[:block] for pair in pairs_y]
            + [pair[block : 2 * block] for pair in pairs_y]
            + [pairs_y[-1][2 * block :]],
            axis=0,
        )
    blocks = [gather_block(*bounds[0]), gather_block(*bounds[1], here[2])]
    mix = [whole, swap(whole, "tensor", 1), whole_y, swap(whole_y, "tensor", 1)]

    lane = jnp.arange(width, dtype=jnp.int32)
    order = blocks_order()[0]
    source = jnp.repeat(order, block) * block + lane % block
    perm = (lane[:, None] == source[None, :]).astype(BF)
    perm_back = (source[:, None] == lane[None, :]).astype(BF)
    doc_ids = after(doc_ids, here[-1])
    last = doc_ids.shape[0]
    ids = jnp.concatenate([doc_ids[:1], doc_ids[:1], doc_ids, doc_ids[last - 1 :], doc_ids[last - 1 :]])
    ids = lax.dynamic_slice(ids, (me_t * rows,), (rows + 4,))
    one_all = (ids[1:] == ids[:-1]).astype(F32)[:, None]
    two_all = (ids[2:] == ids[:-2]).astype(F32)[:, None]
    keep_one, keep_two = one_all[1 : rows + 1], two_all[:rows]
    next_one, next_two = one_all[2 : rows + 2], two_all[2 : rows + 2]
    gain_one, gain_two = gain_mixer.astype(F32), gain_ffn.astype(F32)
    cot = cotangent
    extended = after(jnp.concatenate([halo, tokens_in], axis=0), here[1])
    normed_ext, scale_ext = normalize(extended.astype(F32))
    hidden_ext = reorder((normed_ext * gain_one).astype(BF), perm)
    scale_one = scale_ext[HALO:]
    hidden_one = hidden_ext[HALO:]
    tokens_f = tokens_in.astype(F32)

    saved = []
    mixed = 0.0
    for group in mix:
        taps = group[width : width + 3, :channels].astype(F32)
        projected = nn(hidden_ext, group[:width, : 3 * channels])
        b_part = projected[:, :channels]
        v_part = projected[:, channels : 2 * channels]
        c_part = projected[HALO:, 2 * channels :]
        bx = b_part * v_part
        bx0, bx1, bx2 = bx[HALO:], keep_one * bx[HALO - 1 : -1], keep_two * bx[HALO - 2 : -2]
        conv_out = taps[0] * bx0 + taps[1] * bx1 + taps[2] * bx2
        gated = (c_part * conv_out).astype(BF)
        mixed = mixed + nt(gated, group[:width, 3 * channels :])
        saved.append((b_part[HALO:], c_part, v_part[HALO:], bx0, bx1, bx2, conv_out, gated, taps))
    resid = tokens_f + reorder_f32(mixed, perm_back)
    normed_two, scale_two = normalize(resid)
    hidden_two = (normed_two * gain_two).astype(BF)
    hid_y = swap(hidden_two, "tensor", 2)
    tile = min(rows // 2, 256)

    def weight_grads(d_gu, act, *earlier):
        tokens, grads = lax.optimization_barrier((hid_all, cot_all) + earlier)[:2]
        grads = jnp.concatenate([tn(tokens, d_gu).astype(BF), tn(grads, act).astype(BF)], axis=1)
        return grads, lax.psum_scatter(grads, "dp", scatter_dimension=0, tiled=True)

    hid = [[hidden_two, swap(hidden_two, "tensor", 1)]]
    cots = [[cot, swap(cot, "tensor", 1)]]
    near = ffn(hid[0], cots[0], blocks[0], (), (), 0, tile)
    hid_y, cot_y = lax.optimization_barrier((hid_y, cot_y, near[0]))[:2]
    hid.append([hid_y, swap(hid_y, "tensor", 1)])
    cots.append([cot_y, swap(cot_y, "tensor", 1)])
    far = ffn(hid[1], cots[1], blocks[0], (), tuple(near[4:]), 1, tile)
    hid_all, cot_all = far[6:]
    parts_one, sums_one = weight_grads(*far[4:6], blocks[1])
    hid[1][0] = after(hid[1][0], parts_one)
    far_two = ffn(hid[1], cots[1], blocks[1], tuple(far[:4]), (), 1, tile)
    far_core = [swap(value, "tensor", 1) for value in far_two[2:4]]
    d_far, out_far = (
        (value.astype(F32) + got.astype(F32)).astype(BF) for value, got in zip(far_two, far_core)
    )
    d_y = swap(d_far, "tensor", 2)
    hid[0][0] = after(hid[0][0], far_core[0])
    near_two = ffn(hid[0], cots[0], blocks[1], tuple(near[:4]), tuple(far_two[4:]), 0, tile)
    parts_two, sums_two = weight_grads(*near_two[4:])

    near_core = [swap(value, "tensor", 1) for value in near_two[2:4]]
    d_hidden_two, out_own = (
        value.astype(F32) + got.astype(F32) for value, got in zip(near_two, near_core)
    )
    d_hidden_two = after(d_hidden_two + d_y.astype(F32), parts_two)
    d_resid = cot.astype(F32) + norm_back(d_hidden_two * gain_two, normed_two, scale_two)
    d_mix = reorder(d_resid.astype(BF), perm)

    d_gated = [nn(d_mix, group[:width, 3 * channels :]) for group in mix]
    d_conv = [back * keep[1] for back, keep in zip(d_gated, saved)]
    first = jnp.stack(by_xor([value[:2] for value in d_conv], me_t))
    following = shift(first, -1)
    following = by_xor([following[i] for i in range(4)], me_t)

    def add_z(sums):
        return sum(
            [sums[0]] + [ring(sums[k].astype(BF), "dp", -2 * k).astype(F32) for k in range(1, deep)]
        )

    d_cs = [(d_gated[r] * saved[r][6]).astype(BF) for r in range(4)]

    def sides(values, r):
        return jnp.concatenate([values[r], values[r + 2]], axis=1)

    gates = [saved[r][7] for r in range(4)]
    right = [
        jnp.concatenate(
            [tn(hidden_one, sides(d_cs, r)).astype(BF), tn(d_mix, sides(gates, r)).astype(BF)], axis=1
        )
        for r in (1, 0)
    ]
    right_core = swap(right[0], "tensor", 1)

    d_bvs = []
    for r in range(4):
        b_part, c_part, v_part, bx0, bx1, bx2, conv_out, gated, taps = saved[r]
        ahead = jnp.concatenate([d_conv[r], following[r]], axis=0)
        d_bx = (
            taps[0] * d_conv[r]
            + taps[1] * next_one * ahead[1 : rows + 1]
            + taps[2] * next_two * ahead[2:]
        )
        d_bvs.append(jnp.concatenate([d_bx * v_part, d_bx * b_part], axis=1).astype(BF))
    hidden_late = after(hidden_one, *right)
    left = [tn(hidden_late, sides(d_bvs, r)).astype(BF) for r in (1, 0)]
    left_core = swap(left[0], "tensor", 1)

    side = 2 * channels
    right_all = right[1].astype(F32) + right_core.astype(F32)
    right_near, right_far = (
        jnp.concatenate([right_all[:, i : i + channels], right_all[:, i + side : i + side + channels]], axis=1)
        for i in (0, channels)
    )
    left_all = left[1].astype(F32) + left_core.astype(F32)
    left_near, left_far = left_all[:, :side], left_all[:, side:]
    left_far = left_far.astype(BF)
    left_y = swap(left_far, "tensor", 2)
    left_sum = left_near + left_y.astype(F32)
    if long:
        right_sum = right_near + swap(right_far.astype(BF), "tensor", 2).astype(F32)
        total = jnp.concatenate([left_sum, right_sum], axis=1).astype(BF)
        mix_sum = long_scatter(total[:half], total[half:])
        d_late = d_cs
    else:
        right_x = swap(jnp.concatenate([right_near[half:], right_far[half:]], axis=0).astype(BF), "dp", 1)
        right_x = after(right_x, left_y)
        right_near = right_near[:half] + right_x[:half].astype(F32)
        right_far = right_far[:half] + right_x[half:].astype(F32)
        right_sum = right_near + swap(right_far.astype(BF), "tensor", 2).astype(F32)
        left_sum = left_sum[:half] + swap(left_sum[half:].astype(BF), "dp", 1).astype(F32)
        total = jnp.concatenate([left_sum, right_sum], axis=1).reshape(deep, block, -1)
        mix_sum = add_z(total)
        d_late = lax.optimization_barrier((d_cs, left_far))[0]

    out_y = swap(after(out_far, right_sum), "tensor", 2)
    block_out = (resid + (out_own + out_y.astype(F32))).astype(BF)
    d_hidden_one = 0.0
    for r, group in enumerate(mix):
        d_proj = jnp.concatenate([d_bvs[r], d_late[r]], axis=1)
        d_hidden_one = d_hidden_one + nt(d_proj, group[:width, : 3 * channels])
    d_hidden_one = reorder_f32(d_hidden_one, perm_back)
    normed_one = tokens_f * scale_one
    part_gain_one = jnp.sum(d_hidden_one * normed_one, axis=0)
    part_gain_two = jnp.sum(d_hidden_two * normed_two, axis=0)
    grad_input = d_resid + norm_back(d_hidden_one * gain_one, normed_one, scale_one)

    conv_parts = [
        jnp.stack([jnp.sum(value * d_conv[r], axis=0) for value in saved[r][3:6]]) for r in range(4)
    ]
    conv_all = jnp.stack(by_xor(conv_parts, me_t), axis=1)
    gain_parts = jnp.stack([part_gain_one, part_gain_two])
    small = jnp.concatenate([gain_parts, conv_all.reshape(-1, width)], axis=0)
    if long:
        small = lax.psum(small, ("dp", "tensor"))
    else:
        small = small + swap(small, "tensor", 1)
        bit = deep // 2
        while bit:
            small = small + ring(small, "dp", 2 * bit)
            bit //= 2
        small = after(small, total)
        got = [swap(small, "dp", 1), swap(small, "tensor", 2), cross(small)]
        small = small + got[0] + got[1] + got[2]
    grad_conv = lax.dynamic_slice(small, (2, me_t * channels), (small.shape[0] - 2, channels))

    grad_in = jnp.stack([mix_sum[:, i * channels : (i + 1) * channels] for i in (0, 2, 1)], axis=1)
    grad_out = mix_sum[:, 3 * channels :].T
    grad_gu, grad_down = [], []
    for part, (lo, hi) in zip((sums_one.astype(F32), sums_two.astype(F32)), bounds):
        size = hi - lo
        grad_gu.append(part[:, : 2 * size].reshape(block, 2, size))
        grad_down.append(part[:, 2 * size :].T)
    return (
        block_out,
        grad_input,
        small[0],
        grad_in,
        grad_conv,
        grad_out,
        small[1],
        jnp.concatenate(grad_gu, axis=2),
        jnp.concatenate(grad_down, axis=0),
    )


def solution(mesh):
    return jax.shard_map(
        body,
        mesh=mesh,
        in_specs=(
            P(("dp", "tensor"), None),
            P("dp"),
            P(),
            P("dp", None, "tensor"),
            P(None, "tensor"),
            P("tensor", "dp"),
            P(),
            P("dp", None, "tensor"),
            P("tensor", "dp"),
            P(("dp", "tensor"), None),
        ),
        out_specs=(
            P(("dp", "tensor"), None),
            P(("dp", "tensor"), None),
            P(),
            P("dp", None, "tensor"),
            P(None, "tensor"),
            P("tensor", "dp"),
            P(),
            P("dp", None, "tensor"),
            P("tensor", "dp"),
        ),
        check_vma=False,
    )
```

```python
import jax
import jax.numpy as jnp
from jax import lax
from jax.experimental import pallas as pl
from jax.experimental.pallas import tpu as pltpu
from jax.sharding import PartitionSpec as P

epsilon = 1e-05
HALO = 16
LONG = 8
BF = jnp.bfloat16
F32 = jnp.float32


def swap(value, axis, bit):
    peers = lax.axis_size(axis)
    return lax.ppermute(value, axis, [(i, i ^ bit) for i in range(peers)])


def ring(value, axis, by):
    peers = lax.axis_size(axis)
    return lax.ppermute(value, axis, [(i, (i + by) % peers) for i in range(peers)])


def shift(value, by):
    peers = lax.axis_size("dp") * lax.axis_size("tensor")
    pairs = [(i, i + by) for i in range(peers) if 0 <= i + by < peers]
    return lax.ppermute(value, ("dp", "tensor"), pairs)


def cross(value):
    inner = lax.axis_size("tensor")
    peers = lax.axis_size("dp") * inner
    return lax.ppermute(value, ("dp", "tensor"), [(i, i ^ (inner + 2)) for i in range(peers)])


def nn(left, right):
    return jnp.dot(left, right, preferred_element_type=F32)


def tn(left, right):
    return lax.dot_general(left, right, (((0,), (0,)), ((), ())), preferred_element_type=F32)


def nt(left, right):
    return lax.dot_general(left, right, (((1,), (1,)), ((), ())), preferred_element_type=F32)


def normalize(values):
    scale_vec = lax.rsqrt(jnp.mean(values * values, axis=-1, keepdims=True) + epsilon)
    return (values * scale_vec, scale_vec)


def norm_back(d_normed, normed, scale_vec):
    return scale_vec * (d_normed - normed * jnp.mean(d_normed * normed, axis=-1, keepdims=True))


def after(value, *others):
    return lax.optimization_barrier((value,) + others)[0]


def reorder(values, perm):
    return nn(values, perm).astype(BF)


def reorder_f32(values, perm):
    high = lax.optimization_barrier(values.astype(BF))
    low = (values - high.astype(F32)).astype(BF)
    return nn(high, perm) + nn(low, perm)


def blocks_order():
    steps, me = lax.axis_size("dp") // 2, lax.axis_index("dp")
    index = jnp.arange(2 * steps, dtype=jnp.int32)
    order = ((me // 2 - index % steps) % steps) * 2 + ((me % 2) ^ (index // steps))
    inverse = ((index % 2) ^ (me % 2)) * steps + (me // 2 - index // 2) % steps
    return order, inverse


def long_gather(shard):
    whole = lax.all_gather(shard, "dp", axis=0)[blocks_order()[0]]
    return whole.reshape(-1, shard.shape[1])


def long_scatter(near, far):
    total = jnp.concatenate([near, far], axis=0)
    peers = lax.axis_size("dp")
    total = total.reshape(peers, total.shape[0] // peers, -1)[blocks_order()[1]].reshape(total.shape)
    return lax.psum_scatter(total, "dp", scatter_dimension=0, tiled=True).astype(F32)


def chain(shard):
    here = [shard]
    for _ in range(lax.axis_size("dp") // 2 - 1):
        here.append(ring(here[-1], "dp", 2))
    return here


def others(here):
    return [swap(piece, "dp", 1) for piece in here]


def ffn(hidden, cot, weights, before, kept, part, tile):
    slot_rows, width = hidden[0].shape
    rows = 2 * slot_rows
    size = weights.shape[1] // 3
    steps = rows // tile
    skip = part * steps
    wide = [2 * size, size] + ([] if before else [width, width])

    def kernel(*refs):
        slots, w_ref, refs = refs[:4], refs[4], refs[5:]
        if before:
            h_ref, g_ref = refs[-2:]
            refs = refs[:-2]
        else:
            h_ref, g_ref = refs[-2:]
        outs = refs[len(before) + len(kept) :]
        d_gu_ref, act_ref = outs[4:6]

        def at(slot):
            return pl.when(pl.program_id(0) // (steps // 2) == slot)

        for slot in (0, 1):

            @at(slot)
            def _(slot=slot):
                h_ref[...] = slots[slot][...]
                g_ref[...] = slots[2 + slot][...]

        gate_up = nn(h_ref[...], w_ref[:, : 2 * size])
        d_act = nn(g_ref[...], w_ref[:, 2 * size :])
        gate, up = gate_up[:, :size], gate_up[:, size:]
        sigma = 1.0 / (1.0 + jnp.exp(-gate))
        silu = gate * sigma
        act = (silu * up).astype(BF)
        act_ref[...] = act
        d_gu_ref[:, :size] = (d_act * up * (sigma * (1.0 + gate * (1.0 - sigma)))).astype(BF)
        d_gu_ref[:, size:] = (d_act * silu).astype(BF)
        sums = [nt(d_gu_ref[...], w_ref[:, : 2 * size]), nt(act, w_ref[:, 2 * size :])]
        for slot in (0, 1):

            @at(slot)
            def _(slot=slot):
                for i, value in enumerate(sums):
                    at_ref = outs[2 * slot + i]
                    if before:
                        value = value + refs[2 * slot + i][...]
                    at_ref[...] = value.astype(at_ref.dtype)

    whole = pl.BlockSpec(memory_space=pl.ANY)
    near = pl.BlockSpec((tile, width), lambda i: (jnp.minimum(i, steps // 2 - 1), 0))
    far = pl.BlockSpec((tile, width), lambda i: (jnp.maximum(i - steps // 2, 0), 0))
    kind = BF if before else F32
    aliased = 5 + len(before)
    return pl.pallas_call(
        kernel,
        grid=(steps,),
        in_specs=[near, far] * 2
        + [pl.BlockSpec(weights.shape, lambda i: (0, 0))]
        + [near, near, far, far][: len(before)]
        + [whole] * len(kept),
        out_specs=[near, near, far, far] + [pl.BlockSpec((tile, n), lambda i: (i + skip, 0)) for n in wide],
        out_shape=[jax.ShapeDtypeStruct((slot_rows, width), kind)] * 4
        + [jax.ShapeDtypeStruct((2 * rows, n), BF) for n in wide],
        scratch_shapes=[pltpu.VMEM((tile, width), BF)] * (2 if before else 0),
        input_output_aliases={aliased + i: 4 + i for i in range(len(kept))},
        compiler_params=pltpu.CompilerParams(vmem_limit_bytes=48 << 20),
        cost_estimate=pl.CostEstimate(
            flops=12 * rows * width * size,
            bytes_accessed=rows * width * 12 + width * size * 6,
            transcendentals=rows * size,
        ),
    )(*hidden, *cot, weights, *before, *kept)


def by_xor(groups, me):
    one = [jnp.where((me & 1) == 1, groups[i ^ 1], groups[i]) for i in range(4)]
    return [jnp.where((me & 2) == 2, one[i ^ 2], one[i]) for i in range(4)]


def body(
    tokens_in,
    doc_ids,
    gain_mixer,
    in_weight,
    conv_weight,
    out_weight,
    gain_ffn,
    gate_up_weight,
    down_weight,
    cotangent,
):
    rows, width = tokens_in.shape
    dp_count = lax.axis_size("dp")
    block = width // dp_count
    channels = in_weight.shape[2]
    units = gate_up_weight.shape[2]
    me_t = lax.axis_index("tensor")
    deep = dp_count // 2
    half = width // 2
    long = deep > LONG

    tail = tokens_in[rows - HALO :]
    linked = (doc_ids[(me_t + 1) * rows - 2] == doc_ids[(me_t + 1) * rows - 1]).astype(BF)
    tail = tail * jnp.ones((HALO, 1), BF).at[HALO - 2, 0].set(linked)
    halo = shift(tail, 1)

    packed = jnp.concatenate(
        [in_weight[:, 0], in_weight[:, 2], in_weight[:, 1], out_weight.T], axis=1
    )
    taps_rows = jnp.zeros((HALO, 4 * channels), BF).at[:3, :channels].set(conv_weight)
    cut = units // 2 // 128 * 128
    bounds = [(0, cut), (cut, units)]


    def gather_block(lo, hi, *earlier):
        gate_up, down = lax.optimization_barrier((gate_up_weight, down_weight) + earlier)[:2]
        shard = jnp.concatenate([gate_up[:, 0, lo:hi], gate_up[:, 1, lo:hi], down[lo:hi].T], axis=1)
        return lax.all_gather(shard, "dp", axis=0, tiled=True)

    early, later = cotangent[: rows // 2], cotangent[rows // 2 :]
    cot_y = [swap(after(early, halo), "tensor", 2)]
    if long:
        whole = jnp.concatenate([long_gather(packed), taps_rows], axis=0)
        whole_y = swap(whole, "tensor", 2)
        here = [packed] * 3
    else:
        here = chain(packed)
        across = others(here)
        sent = [[here[k], across[k]] for k in range(deep // 2)]
        sent += [here[deep // 2 :], across[deep // 2 :] + [taps_rows]]
        got = [swap(jnp.concatenate(pieces, axis=0), "tensor", 2) for pieces in sent]
        whole = jnp.concatenate(here + across + [taps_rows], axis=0)
        near, far = got[: deep // 2], got[deep // 2 :]
        whole_y = jnp.concatenate(
            [pair[:block] for pair in near] + [far[0]] + [pair[block:] for pair in near] + [far[1]], axis=0
        )
    blocks = [gather_block(*bounds[0]), gather_block(*bounds[1], here[2])]
    cot_y.append(swap(after(later, whole_y), "tensor", 2))
    mix = [whole, swap(whole, "tensor", 1), whole_y, swap(whole_y, "tensor", 1)]

    lane = jnp.arange(width, dtype=jnp.int32)
    order = blocks_order()[0]
    source = jnp.repeat(order, block) * block + lane % block
    perm = (lane[:, None] == source[None, :]).astype(BF)
    perm_back = (source[:, None] == lane[None, :]).astype(BF)
    doc_ids = after(doc_ids, here[-1])
    last = doc_ids.shape[0]
    ids = jnp.concatenate([doc_ids[:1], doc_ids[:1], doc_ids, doc_ids[last - 1 :], doc_ids[last - 1 :]])
    ids = lax.dynamic_slice(ids, (me_t * rows,), (rows + 4,))
    one_all = (ids[1:] == ids[:-1]).astype(F32)[:, None]
    two_all = (ids[2:] == ids[:-2]).astype(F32)[:, None]
    keep_one, keep_two = one_all[1 : rows + 1], two_all[:rows]
    next_one, next_two = one_all[2 : rows + 2], two_all[2 : rows + 2]
    gain_one, gain_two = gain_mixer.astype(F32), gain_ffn.astype(F32)
    cot = cotangent
    extended = after(jnp.concatenate([halo, tokens_in], axis=0), here[1])
    normed_ext, scale_ext = normalize(extended.astype(F32))
    hidden_ext = reorder((normed_ext * gain_one).astype(BF), perm)
    scale_one = scale_ext[HALO:]
    hidden_one = hidden_ext[HALO:]
    tokens_f = tokens_in.astype(F32)

    saved = []
    mixed = 0.0
    for group in mix:
        taps = group[width : width + 3, :channels].astype(F32)
        projected = nn(hidden_ext, group[:width, : 3 * channels])
        b_part = projected[:, :channels]
        v_part = projected[:, channels : 2 * channels]
        c_part = projected[HALO:, 2 * channels :]
        bx = b_part * v_part
        bx0, bx1, bx2 = bx[HALO:], keep_one * bx[HALO - 1 : -1], keep_two * bx[HALO - 2 : -2]
        conv_out = taps[0] * bx0 + taps[1] * bx1 + taps[2] * bx2
        gated = (c_part * conv_out).astype(BF)
        mixed = mixed + nt(gated, group[:width, 3 * channels :])
        saved.append((b_part[HALO:], c_part, v_part[HALO:], bx0, bx1, bx2, conv_out, gated, taps))
    resid = tokens_f + reorder_f32(mixed, perm_back)
    normed_two, scale_two = normalize(resid)
    hidden_two = (normed_two * gain_two).astype(BF)
    cot_y = jnp.concatenate(cot_y, axis=0)
    hid_y = swap(after(hidden_two, cot_y), "tensor", 2)
    tile = min(rows // 2, 256)

    def weight_grads(d_gu, act, *earlier):
        grad_gu = tn(hid_all, d_gu).astype(BF)
        grads = after(cot_all, grad_gu, *earlier)
        grads = jnp.concatenate([grad_gu, tn(grads, act).astype(BF)], axis=1)
        return grads, lax.psum_scatter(grads, "dp", scatter_dimension=0, tiled=True)

    hid = [[hidden_two, swap(hidden_two, "tensor", 1)]]
    cots = [[cot, swap(after(cot, whole), "tensor", 1)]]
    near = ffn(hid[0], cots[0], blocks[0], (), (), 0, tile)
    hid_y, cot_y = lax.optimization_barrier((hid_y, cot_y, near[0]))[:2]
    hid.append([hid_y, swap(hid_y, "tensor", 1)])
    cots.append([cot_y, swap(cot_y, "tensor", 1)])
    far = ffn(hid[1], cots[1], blocks[0], (), tuple(near[4:]), 1, tile)
    hid_all, cot_all = far[6:]
    parts_one, sums_one = weight_grads(*far[4:6], blocks[1])
    hid[1][0] = after(hid[1][0], parts_one)
    far_two = ffn(hid[1], cots[1], blocks[1], tuple(far[:4]), (), 1, tile)
    far_core = [swap(value, "tensor", 1) for value in far_two[2:4]]
    d_far, out_far = (
        (value.astype(F32) + got.astype(F32)).astype(BF) for value, got in zip(far_two, far_core)
    )
    d_y = swap(d_far, "tensor", 2)
    hid[0][0] = after(hid[0][0], far_core[0])
    near_two = ffn(hid[0], cots[0], blocks[1], tuple(near[:4]), tuple(far_two[4:]), 0, tile)
    parts_two, sums_two = weight_grads(*near_two[4:])

    near_core = [swap(value, "tensor", 1) for value in near_two[2:4]]
    d_hidden_two, out_own = (
        value.astype(F32) + got.astype(F32) for value, got in zip(near_two, near_core)
    )
    d_hidden_two = after(d_hidden_two + d_y.astype(F32), parts_two)
    d_resid = cot.astype(F32) + norm_back(d_hidden_two * gain_two, normed_two, scale_two)
    d_mix = reorder(d_resid.astype(BF), perm)

    d_gated = [nn(d_mix, group[:width, 3 * channels :]) for group in mix]
    d_conv = [back * keep[1] for back, keep in zip(d_gated, saved)]
    first = jnp.stack(by_xor([value[:2] for value in d_conv], me_t))
    following = shift(first, -1)
    following = by_xor([following[i] for i in range(4)], me_t)

    d_cs = [(d_gated[r] * saved[r][6]).astype(BF) for r in range(4)]

    def sides(values, r):
        return jnp.concatenate([values[r], values[r + 2]], axis=1)

    gates = [saved[r][7] for r in range(4)]
    right = [
        jnp.concatenate(
            [tn(hidden_one, sides(d_cs, r)).astype(BF), tn(d_mix, sides(gates, r)).astype(BF)], axis=1
        )
        for r in (1, 0)
    ]
    right_core = swap(right[0], "tensor", 1)

    d_bvs = []
    for r in range(4):
        b_part, c_part, v_part, bx0, bx1, bx2, conv_out, gated, taps = saved[r]
        ahead = jnp.concatenate([d_conv[r], following[r]], axis=0)
        d_bx = (
            taps[0] * d_conv[r]
            + taps[1] * next_one * ahead[1 : rows + 1]
            + taps[2] * next_two * ahead[2:]
        )
        d_bvs.append(jnp.concatenate([d_bx * v_part, d_bx * b_part], axis=1).astype(BF))
    hidden_late = after(hidden_one, *right)
    left = [tn(hidden_late, sides(d_bvs, r)).astype(BF) for r in (1, 0)]
    left_core = swap(left[0], "tensor", 1)

    side = 2 * channels
    right_all = right[1].astype(F32) + right_core.astype(F32)
    right_near, right_far = (
        jnp.concatenate([right_all[:, i : i + channels], right_all[:, i + side : i + side + channels]], axis=1)
        for i in (0, channels)
    )
    left_all = left[1].astype(F32) + left_core.astype(F32)
    left_near, left_far = left_all[:, :side], left_all[:, side:]
    left_far = left_far.astype(BF)
    left_y = swap(left_far, "tensor", 2)
    left_sum = left_near + left_y.astype(F32)
    if long:
        right_sum = right_near + swap(right_far.astype(BF), "tensor", 2).astype(F32)
        total = jnp.concatenate([left_sum, right_sum], axis=1).astype(BF)
        mix_sum = long_scatter(total[:half], total[half:])
        d_late = d_cs
        block_out = (resid + (out_own + swap(out_far, "tensor", 2).astype(F32))).astype(BF)
    else:
        right_x = swap(jnp.concatenate([right_near[half:], right_far[half:]], axis=0).astype(BF), "dp", 1)
        right_x = after(right_x, left_y)
        right_near = right_near[:half] + right_x[:half].astype(F32)
        right_far = right_far[:half] + right_x[half:].astype(F32)
        right_sum = right_near + swap(right_far.astype(BF), "tensor", 2).astype(F32)
        left_sum = left_sum[:half] + swap(left_sum[half:].astype(BF), "dp", 1).astype(F32)
        total = jnp.concatenate([left_sum, right_sum], axis=1).reshape(deep, block, -1)
        got = [ring(total[k].astype(BF), "dp", -2 * k) for k in range(1, deep)]
        out_y = swap(after(out_far, right_sum), "tensor", 2)
        block_out = (resid + (out_own + out_y.astype(F32))).astype(BF)
        got = lax.optimization_barrier((*got, block_out))[:-1]
        mix_sum = sum([total[0]] + [piece.astype(F32) for piece in got])
        d_late = lax.optimization_barrier((d_cs, left_far))[0]

    d_hidden_one = 0.0
    for r, group in enumerate(mix):
        d_proj = jnp.concatenate([d_bvs[r], d_late[r]], axis=1)
        d_hidden_one = d_hidden_one + nt(d_proj, group[:width, : 3 * channels])
    d_hidden_one = reorder_f32(d_hidden_one, perm_back)
    normed_one = tokens_f * scale_one
    part_gain_one = jnp.sum(d_hidden_one * normed_one, axis=0)
    part_gain_two = jnp.sum(d_hidden_two * normed_two, axis=0)
    grad_input = d_resid + norm_back(d_hidden_one * gain_one, normed_one, scale_one)

    conv_parts = [
        jnp.stack([jnp.sum(value * d_conv[r], axis=0) for value in saved[r][3:6]]) for r in range(4)
    ]
    conv_all = jnp.stack(by_xor(conv_parts, me_t), axis=1)
    gain_parts = jnp.stack([part_gain_one, part_gain_two])
    small = jnp.concatenate([gain_parts, conv_all.reshape(-1, width)], axis=0)
    if long:
        small = lax.psum(small, ("dp", "tensor"))
    else:
        small = small + swap(small, "tensor", 1)
        bit = deep // 2
        while bit:
            small = small + ring(small, "dp", 2 * bit)
            bit //= 2
        small = after(small, total)
        got = [swap(small, "dp", 1), swap(small, "tensor", 2), cross(small)]
        small = small + got[0] + got[1] + got[2]
    grad_conv = lax.dynamic_slice(small, (2, me_t * channels), (small.shape[0] - 2, channels))

    grad_in = jnp.stack([mix_sum[:, i * channels : (i + 1) * channels] for i in (0, 2, 1)], axis=1)
    grad_out = mix_sum[:, 3 * channels :].T
    grad_gu, grad_down = [], []
    for part, (lo, hi) in zip((sums_one.astype(F32), sums_two.astype(F32)), bounds):
        size = hi - lo
        grad_gu.append(part[:, : 2 * size].reshape(block, 2, size))
        grad_down.append(part[:, 2 * size :].T)
    return (
        block_out,
        grad_input,
        small[0],
        grad_in,
        grad_conv,
        grad_out,
        small[1],
        jnp.concatenate(grad_gu, axis=2),
        jnp.concatenate(grad_down, axis=0),
    )


def solution(mesh):
    return jax.shard_map(
        body,
        mesh=mesh,
        in_specs=(
            P(("dp", "tensor"), None),
            P("dp"),
            P(),
            P("dp", None, "tensor"),
            P(None, "tensor"),
            P("tensor", "dp"),
            P(),
            P("dp", None, "tensor"),
            P("tensor", "dp"),
            P(("dp", "tensor"), None),
        ),
        out_specs=(
            P(("dp", "tensor"), None),
            P(("dp", "tensor"), None),
            P(),
            P("dp", None, "tensor"),
            P(None, "tensor"),
            P("tensor", "dp"),
            P(),
            P("dp", None, "tensor"),
            P("tensor", "dp"),
        ),
        check_vma=False,
    )
```

```python
import jax
import jax.numpy as jnp
from jax import lax
from jax.experimental import pallas as pl
from jax.experimental.pallas import tpu as pltpu
from jax.sharding import PartitionSpec as P

epsilon = 1e-05
HALO = 16
LONG = 8
BF = jnp.bfloat16
F32 = jnp.float32


def swap(value, axis, bit):
    peers = lax.axis_size(axis)
    return lax.ppermute(value, axis, [(i, i ^ bit) for i in range(peers)])


def ring(value, axis, by):
    peers = lax.axis_size(axis)
    return lax.ppermute(value, axis, [(i, (i + by) % peers) for i in range(peers)])


def shift(value, by):
    peers = lax.axis_size("dp") * lax.axis_size("tensor")
    pairs = [(i, i + by) for i in range(peers) if 0 <= i + by < peers]
    return lax.ppermute(value, ("dp", "tensor"), pairs)


def cross(value):
    inner = lax.axis_size("tensor")
    peers = lax.axis_size("dp") * inner
    return lax.ppermute(value, ("dp", "tensor"), [(i, i ^ (inner + 2)) for i in range(peers)])


def nn(left, right):
    return jnp.dot(left, right, preferred_element_type=F32)


def tn(left, right):
    return lax.dot_general(left, right, (((0,), (0,)), ((), ())), preferred_element_type=F32)


def nt(left, right):
    return lax.dot_general(left, right, (((1,), (1,)), ((), ())), preferred_element_type=F32)


def normalize(values):
    scale_vec = lax.rsqrt(jnp.mean(values * values, axis=-1, keepdims=True) + epsilon)
    return (values * scale_vec, scale_vec)


def norm_back(d_normed, normed, scale_vec):
    return scale_vec * (d_normed - normed * jnp.mean(d_normed * normed, axis=-1, keepdims=True))


def after(value, *others):
    return lax.optimization_barrier((value,) + others)[0]


def reorder(values, perm):
    return nn(values, perm).astype(BF)


def reorder_f32(values, perm):
    high = lax.optimization_barrier(values.astype(BF))
    low = (values - high.astype(F32)).astype(BF)
    return nn(high, perm) + nn(low, perm)


def blocks_order():
    steps, me = lax.axis_size("dp") // 2, lax.axis_index("dp")
    index = jnp.arange(2 * steps, dtype=jnp.int32)
    order = ((me // 2 - index % steps) % steps) * 2 + ((me % 2) ^ (index // steps))
    inverse = ((index % 2) ^ (me % 2)) * steps + (me // 2 - index // 2) % steps
    return order, inverse


def long_gather(shard):
    whole = lax.all_gather(shard, "dp", axis=0)[blocks_order()[0]]
    return whole.reshape(-1, shard.shape[1])


def long_scatter(near, far):
    total = jnp.concatenate([near, far], axis=0)
    peers = lax.axis_size("dp")
    total = total.reshape(peers, total.shape[0] // peers, -1)[blocks_order()[1]].reshape(total.shape)
    return lax.psum_scatter(total, "dp", scatter_dimension=0, tiled=True).astype(F32)


def chain(shard):
    here = [shard]
    for _ in range(lax.axis_size("dp") // 2 - 1):
        here.append(ring(here[-1], "dp", 2))
    return here


def others(here):
    return [swap(piece, "dp", 1) for piece in here]


def ffn(hidden, cot, weights, before, kept, part, tile):
    slot_rows, width = hidden[0].shape
    rows = 2 * slot_rows
    size = weights.shape[1] // 3
    steps = rows // tile
    skip = part * steps
    wide = [2 * size, size] + ([] if before else [width, width])

    def kernel(*refs):
        slots, w_ref, refs = refs[:4], refs[4], refs[5:]
        if before:
            h_ref, g_ref = refs[-2:]
            refs = refs[:-2]
        else:
            h_ref, g_ref = refs[-2:]
        outs = refs[len(before) + len(kept) :]
        d_gu_ref, act_ref = outs[4:6]

        def at(slot):
            return pl.when(pl.program_id(0) // (steps // 2) == slot)

        for slot in (0, 1):

            @at(slot)
            def _(slot=slot):
                h_ref[...] = slots[slot][...]
                g_ref[...] = slots[2 + slot][...]

        gate_up = nn(h_ref[...], w_ref[:, : 2 * size])
        d_act = nn(g_ref[...], w_ref[:, 2 * size :])
        gate, up = gate_up[:, :size], gate_up[:, size:]
        sigma = 1.0 / (1.0 + jnp.exp(-gate))
        silu = gate * sigma
        act = (silu * up).astype(BF)
        act_ref[...] = act
        d_gu_ref[:, :size] = (d_act * up * (sigma * (1.0 + gate * (1.0 - sigma)))).astype(BF)
        d_gu_ref[:, size:] = (d_act * silu).astype(BF)
        sums = [nt(d_gu_ref[...], w_ref[:, : 2 * size]), nt(act, w_ref[:, 2 * size :])]
        for slot in (0, 1):

            @at(slot)
            def _(slot=slot):
                for i, value in enumerate(sums):
                    at_ref = outs[2 * slot + i]
                    if before:
                        value = value + refs[2 * slot + i][...]
                    at_ref[...] = value.astype(at_ref.dtype)

    whole = pl.BlockSpec(memory_space=pl.ANY)
    near = pl.BlockSpec((tile, width), lambda i: (jnp.minimum(i, steps // 2 - 1), 0))
    far = pl.BlockSpec((tile, width), lambda i: (jnp.maximum(i - steps // 2, 0), 0))
    kind = BF if before else F32
    aliased = 5 + len(before)
    return pl.pallas_call(
        kernel,
        grid=(steps,),
        in_specs=[near, far] * 2
        + [pl.BlockSpec(weights.shape, lambda i: (0, 0))]
        + [near, near, far, far][: len(before)]
        + [whole] * len(kept),
        out_specs=[near, near, far, far] + [pl.BlockSpec((tile, n), lambda i: (i + skip, 0)) for n in wide],
        out_shape=[jax.ShapeDtypeStruct((slot_rows, width), kind)] * 4
        + [jax.ShapeDtypeStruct((2 * rows, n), BF) for n in wide],
        scratch_shapes=[pltpu.VMEM((tile, width), BF)] * (2 if before else 0),
        input_output_aliases={aliased + i: 4 + i for i in range(len(kept))},
        compiler_params=pltpu.CompilerParams(vmem_limit_bytes=48 << 20),
        cost_estimate=pl.CostEstimate(
            flops=12 * rows * width * size,
            bytes_accessed=rows * width * 12 + width * size * 6,
            transcendentals=rows * size,
        ),
    )(*hidden, *cot, weights, *before, *kept)


def by_xor(groups, me):
    one = [jnp.where((me & 1) == 1, groups[i ^ 1], groups[i]) for i in range(4)]
    return [jnp.where((me & 2) == 2, one[i ^ 2], one[i]) for i in range(4)]


def body(
    tokens_in,
    doc_ids,
    gain_mixer,
    in_weight,
    conv_weight,
    out_weight,
    gain_ffn,
    gate_up_weight,
    down_weight,
    cotangent,
):
    rows, width = tokens_in.shape
    dp_count = lax.axis_size("dp")
    block = width // dp_count
    channels = in_weight.shape[2]
    units = gate_up_weight.shape[2]
    me_t = lax.axis_index("tensor")
    deep = dp_count // 2
    half = width // 2
    long = deep > LONG

    tail = tokens_in[rows - HALO :]
    linked = (doc_ids[(me_t + 1) * rows - 2] == doc_ids[(me_t + 1) * rows - 1]).astype(BF)
    tail = tail * jnp.ones((HALO, 1), BF).at[HALO - 2, 0].set(linked)
    halo = shift(tail, 1)

    packed = jnp.concatenate(
        [in_weight[:, 0], in_weight[:, 2], in_weight[:, 1], out_weight.T], axis=1
    )
    taps_rows = jnp.zeros((HALO, 4 * channels), BF).at[:3, :channels].set(conv_weight)
    cut = units // 2 // 128 * 128
    bounds = [(0, cut), (cut, units)]


    def gather_block(lo, hi, *earlier):
        gate_up, down = lax.optimization_barrier((gate_up_weight, down_weight) + earlier)[:2]
        shard = jnp.concatenate([gate_up[:, 0, lo:hi], gate_up[:, 1, lo:hi], down[lo:hi].T], axis=1)
        return lax.all_gather(shard, "dp", axis=0, tiled=True)

    early, later = cotangent[: rows // 2], cotangent[rows // 2 :]
    cot_y = [swap(after(early, halo), "tensor", 2)]
    if long:
        whole = jnp.concatenate([long_gather(packed), taps_rows], axis=0)
        whole_y = swap(whole, "tensor", 2)
        here = [packed] * 3
    else:
        here = chain(packed)
        across = others(here)
        sent = [[here[k], across[k]] for k in range(deep // 2)]
        sent += [here[deep // 2 :], across[deep // 2 :] + [taps_rows]]
        got = [swap(jnp.concatenate(pieces, axis=0), "tensor", 2) for pieces in sent]
        whole = jnp.concatenate(here + across + [taps_rows], axis=0)
        near, far = got[: deep // 2], got[deep // 2 :]
        whole_y = jnp.concatenate(
            [pair[:block] for pair in near] + [far[0]] + [pair[block:] for pair in near] + [far[1]], axis=0
        )
    blocks = [gather_block(*bounds[0]), gather_block(*bounds[1], here[2])]
    cot_y.append(swap(after(later, whole_y), "tensor", 2))
    mix = [whole, swap(whole, "tensor", 1), whole_y, swap(whole_y, "tensor", 1)]

    lane = jnp.arange(width, dtype=jnp.int32)
    order = blocks_order()[0]
    source = jnp.repeat(order, block) * block + lane % block
    perm = (lane[:, None] == source[None, :]).astype(BF)
    perm_back = (source[:, None] == lane[None, :]).astype(BF)
    doc_ids = after(doc_ids, here[-1])
    last = doc_ids.shape[0]
    ids = jnp.concatenate([doc_ids[:1], doc_ids[:1], doc_ids, doc_ids[last - 1 :], doc_ids[last - 1 :]])
    ids = lax.dynamic_slice(ids, (me_t * rows,), (rows + 4,))
    one_all = (ids[1:] == ids[:-1]).astype(F32)[:, None]
    two_all = (ids[2:] == ids[:-2]).astype(F32)[:, None]
    keep_one, keep_two = one_all[1 : rows + 1], two_all[:rows]
    next_one, next_two = one_all[2 : rows + 2], two_all[2 : rows + 2]
    gain_one, gain_two = gain_mixer.astype(F32), gain_ffn.astype(F32)
    cot = cotangent
    extended = after(jnp.concatenate([halo, tokens_in], axis=0), here[1])
    normed_ext, scale_ext = normalize(extended.astype(F32))
    hidden_ext = reorder((normed_ext * gain_one).astype(BF), perm)
    scale_one = scale_ext[HALO:]
    hidden_one = hidden_ext[HALO:]
    tokens_f = tokens_in.astype(F32)

    saved = []
    mixed = 0.0
    for group in mix:
        taps = group[width : width + 3, :channels].astype(F32)
        projected = nn(hidden_ext, group[:width, : 3 * channels])
        b_part = projected[:, :channels]
        v_part = projected[:, channels : 2 * channels]
        c_part = projected[HALO:, 2 * channels :]
        bx = b_part * v_part
        bx0, bx1, bx2 = bx[HALO:], keep_one * bx[HALO - 1 : -1], keep_two * bx[HALO - 2 : -2]
        conv_out = taps[0] * bx0 + taps[1] * bx1 + taps[2] * bx2
        gated = (c_part * conv_out).astype(BF)
        mixed = mixed + nt(gated, group[:width, 3 * channels :])
        saved.append((b_part[HALO:], c_part, v_part[HALO:], bx0, bx1, bx2, conv_out, gated, taps))
    resid = tokens_f + reorder_f32(mixed, perm_back)
    normed_two, scale_two = normalize(resid)
    hidden_two = (normed_two * gain_two).astype(BF)
    cot_y = jnp.concatenate(cot_y, axis=0)
    hid_y = swap(after(hidden_two, cot_y), "tensor", 2)
    tile = min(rows // 2, 256)

    def weight_grads(d_gu, act, *late):
        if late:
            grad_down = tn(cot_all, act).astype(BF)
            grad_gu = tn(after(hid_all, grad_down), d_gu).astype(BF)
        else:
            grad_gu = tn(hid_all, d_gu).astype(BF)
            grad_down = tn(after(cot_all, grad_gu), act).astype(BF)
        grads = after(jnp.concatenate([grad_gu, grad_down], axis=1), *late)
        return grads, lax.psum_scatter(grads, "dp", scatter_dimension=0, tiled=True)

    hid = [[hidden_two, swap(hidden_two, "tensor", 1)]]
    cots = [[cot, swap(after(cot, whole), "tensor", 1)]]
    near = ffn(hid[0], cots[0], blocks[0], (), (), 0, tile)
    hid_y, cot_y = lax.optimization_barrier((hid_y, cot_y, near[0]))[:2]
    hid.append([hid_y, swap(hid_y, "tensor", 1)])
    cots.append([cot_y, swap(cot_y, "tensor", 1)])
    far = ffn(hid[1], cots[1], blocks[0], (), tuple(near[4:]), 1, tile)
    hid_all, cot_all = far[6:]
    parts_one, sums_one = weight_grads(*far[4:6], blocks[1])
    hid[1][0] = after(hid[1][0], parts_one)
    far_two = ffn(hid[1], cots[1], blocks[1], tuple(far[:4]), (), 1, tile)
    far_core = [swap(value, "tensor", 1) for value in far_two[2:4]]
    d_far, out_far = (
        (value.astype(F32) + got.astype(F32)).astype(BF) for value, got in zip(far_two, far_core)
    )
    d_y = swap(d_far, "tensor", 2)
    hid[0][0] = after(hid[0][0], far_core[0])
    near_two = ffn(hid[0], cots[0], blocks[1], tuple(near[:4]), tuple(far_two[4:]), 0, tile)
    parts_two, sums_two = weight_grads(*near_two[4:])

    near_core = [swap(value, "tensor", 1) for value in near_two[2:4]]
    d_hidden_two, out_own = (
        value.astype(F32) + got.astype(F32) for value, got in zip(near_two, near_core)
    )
    d_hidden_two = after(d_hidden_two + d_y.astype(F32), parts_two)
    d_resid = cot.astype(F32) + norm_back(d_hidden_two * gain_two, normed_two, scale_two)
    d_mix = reorder(d_resid.astype(BF), perm)

    d_gated = [nn(d_mix, group[:width, 3 * channels :]) for group in mix]
    d_conv = [back * keep[1] for back, keep in zip(d_gated, saved)]
    first = jnp.stack(by_xor([value[:2] for value in d_conv], me_t))
    following = shift(first, -1)
    following = by_xor([following[i] for i in range(4)], me_t)

    d_cs = [(d_gated[r] * saved[r][6]).astype(BF) for r in range(4)]

    def sides(values, r):
        return jnp.concatenate([values[r], values[r + 2]], axis=1)

    gates = [saved[r][7] for r in range(4)]
    right = [
        jnp.concatenate(
            [tn(hidden_one, sides(d_cs, r)).astype(BF), tn(d_mix, sides(gates, r)).astype(BF)], axis=1
        )
        for r in (1, 0)
    ]
    right_core = swap(right[0], "tensor", 1)

    d_bvs = []
    for r in range(4):
        b_part, c_part, v_part, bx0, bx1, bx2, conv_out, gated, taps = saved[r]
        ahead = jnp.concatenate([d_conv[r], following[r]], axis=0)
        d_bx = (
            taps[0] * d_conv[r]
            + taps[1] * next_one * ahead[1 : rows + 1]
            + taps[2] * next_two * ahead[2:]
        )
        d_bvs.append(jnp.concatenate([d_bx * v_part, d_bx * b_part], axis=1).astype(BF))
    hidden_late = after(hidden_one, *right)
    left = [tn(hidden_late, sides(d_bvs, r)).astype(BF) for r in (1, 0)]
    left_core = swap(left[0], "tensor", 1)

    side = 2 * channels
    right_all = right[1].astype(F32) + right_core.astype(F32)
    right_near, right_far = (
        jnp.concatenate([right_all[:, i : i + channels], right_all[:, i + side : i + side + channels]], axis=1)
        for i in (0, channels)
    )
    left_all = left[1].astype(F32) + left_core.astype(F32)
    left_near, left_far = left_all[:, :side], left_all[:, side:]
    left_far = left_far.astype(BF)
    left_y = swap(left_far, "tensor", 2)
    left_sum = left_near + left_y.astype(F32)
    if long:
        right_sum = right_near + swap(right_far.astype(BF), "tensor", 2).astype(F32)
        total = jnp.concatenate([left_sum, right_sum], axis=1).astype(BF)
        mix_sum = long_scatter(total[:half], total[half:])
        d_late = d_cs
        block_out = (resid + (out_own + swap(out_far, "tensor", 2).astype(F32))).astype(BF)
    else:
        right_x = swap(jnp.concatenate([right_near[half:], right_far[half:]], axis=0).astype(BF), "dp", 1)
        right_x = after(right_x, left_y)
        right_near = right_near[:half] + right_x[:half].astype(F32)
        right_far = right_far[:half] + right_x[half:].astype(F32)
        right_sum = right_near + swap(right_far.astype(BF), "tensor", 2).astype(F32)
        left_sum = left_sum[:half] + swap(left_sum[half:].astype(BF), "dp", 1).astype(F32)
        total = jnp.concatenate([left_sum, right_sum], axis=1).reshape(deep, block, -1)
        got = [ring(total[k].astype(BF), "dp", -2 * k) for k in range(1, deep)]
        out_y = swap(after(out_far, right_sum), "tensor", 2)
        block_out = (resid + (out_own + out_y.astype(F32))).astype(BF)
        got = lax.optimization_barrier((*got, block_out))[:-1]
        mix_sum = sum([total[0]] + [piece.astype(F32) for piece in got])
        d_late = lax.optimization_barrier((d_cs, left_far))[0]

    d_hidden_one = 0.0
    for r, group in enumerate(mix):
        d_proj = jnp.concatenate([d_bvs[r], d_late[r]], axis=1)
        d_hidden_one = d_hidden_one + nt(d_proj, group[:width, : 3 * channels])
    d_hidden_one = reorder_f32(d_hidden_one, perm_back)
    normed_one = tokens_f * scale_one
    part_gain_one = jnp.sum(d_hidden_one * normed_one, axis=0)
    part_gain_two = jnp.sum(d_hidden_two * normed_two, axis=0)
    grad_input = d_resid + norm_back(d_hidden_one * gain_one, normed_one, scale_one)

    conv_parts = [
        jnp.stack([jnp.sum(value * d_conv[r], axis=0) for value in saved[r][3:6]]) for r in range(4)
    ]
    conv_all = jnp.stack(by_xor(conv_parts, me_t), axis=1)
    gain_parts = jnp.stack([part_gain_one, part_gain_two])
    small = jnp.concatenate([gain_parts, conv_all.reshape(-1, width)], axis=0)
    if long:
        small = lax.psum(small, ("dp", "tensor"))
    else:
        small = small + swap(small, "tensor", 1)
        bit = deep // 2
        while bit:
            small = small + ring(small, "dp", 2 * bit)
            bit //= 2
        small = after(small, total)
        got = [swap(small, "dp", 1), swap(small, "tensor", 2), cross(small)]
        small = small + got[0] + got[1] + got[2]
    grad_conv = lax.dynamic_slice(small, (2, me_t * channels), (small.shape[0] - 2, channels))

    grad_in = jnp.stack([mix_sum[:, i * channels : (i + 1) * channels] for i in (0, 2, 1)], axis=1)
    grad_out = mix_sum[:, 3 * channels :].T
    grad_gu, grad_down = [], []
    for part, (lo, hi) in zip((sums_one.astype(F32), sums_two.astype(F32)), bounds):
        size = hi - lo
        grad_gu.append(part[:, : 2 * size].reshape(block, 2, size))
        grad_down.append(part[:, 2 * size :].T)
    return (
        block_out,
        grad_input,
        small[0],
        grad_in,
        grad_conv,
        grad_out,
        small[1],
        jnp.concatenate(grad_gu, axis=2),
        jnp.concatenate(grad_down, axis=0),
    )


def solution(mesh):
    return jax.shard_map(
        body,
        mesh=mesh,
        in_specs=(
            P(("dp", "tensor"), None),
            P("dp"),
            P(),
            P("dp", None, "tensor"),
            P(None, "tensor"),
            P("tensor", "dp"),
            P(),
            P("dp", None, "tensor"),
            P("tensor", "dp"),
            P(("dp", "tensor"), None),
        ),
        out_specs=(
            P(("dp", "tensor"), None),
            P(("dp", "tensor"), None),
            P(),
            P("dp", None, "tensor"),
            P(None, "tensor"),
            P("tensor", "dp"),
            P(),
            P("dp", None, "tensor"),
            P("tensor", "dp"),
        ),
        check_vma=False,
    )
```
